32 devices in a mesh: ha: 4 (over y, x), wa: 8 (over z, core).
Axes of the slice: x: 2, y: 2, z: 4, core: 2. Of those that a mesh axis runs over, the one named last changes fastest.
Arguments:
- field: bfloat16 [192, 512, 256], P('ha', 'wa'), may hold values from -41 to 41
- expand_w: bfloat16 [256, 1024], replicated, may hold values from -0.375 to 0.375
- dw_kernel: float32 [9, 1024], replicated, may hold values from -2 to 2
- project_w: bfloat16 [1024, 256], replicated, may hold values from -0.1875 to 0.1875
- blk_qkv: bfloat16 [256, 768], replicated, may hold values from -0.375 to 0.375
- blk_out: bfloat16 [256, 256], replicated, may hold values from -0.375 to 0.375
- blk_table: float32 [225, 8], replicated, may hold values from -4 to 290
- blk_index: int32 [64, 64], replicated, may hold values from 0 to 224, as said below
- blk_up: bfloat16 [256, 1024], replicated, may hold values from -0.375 to 0.375
- blk_down: bfloat16 [1024, 256], replicated, may hold values from -0.1875 to 0.1875
- grid_qkv: bfloat16 [256, 768], replicated, may hold values from -0.375 to 0.375
- grid_out: bfloat16 [256, 256], replicated, may hold values from -0.375 to 0.375
- grid_table: float32 [225, 8], replicated, may hold values from -4 to 290
- grid_index: int32 [64, 64], replicated, may hold values from 0 to 224, as said below
- grid_up: bfloat16 [256, 1024], replicated, may hold values from -0.375 to 0.375
- grid_down: bfloat16 [1024, 256], replicated, may hold values from -0.1875 to 0.1875
Outputs:
- updated: bfloat16 [192, 512, 256], P('ha', 'wa')
The draws below stay inside these ranges and needn't reach their ends.
Inputs may be any that keep to these rules, and one draw needn't show every extreme that they name: `blk_index`: two entries are equal exactly when their query and key positions differ by the same row and column offsets inside the window. `grid_index`: two entries are equal exactly when their query and key positions differ by the same row and column offsets inside the window.
All inputs are finite; a program needn't handle non-finite values.
Results may differ from the reference program's by a relative error of at most 0.013.
Values may be sent and summed in bfloat16 or wider, within the bound.
A program may use at most 128 MiB of HBM per device.

```python
import math
import jax
import jax.numpy as jnp
from jax import lax

C = 256
HEADS = 8
EXPAND = 1024
FFN = 1024
BUCKETS = 225
H = 192
W = 512


def draw_field(key, part):
    base_key = jax.random.fold_in(key, 3)
    first, second, third = jax.random.split(base_key, 3)
    cell_scale = jnp.exp(jax.random.uniform(second, (H, W, 1), minval=-1.15, maxval=1.15))
    channel_scale = jnp.exp(jax.random.uniform(third, (1, 1, C), minval=-1.15, maxval=1.15))
    base = jnp.clip(jax.random.normal(first, (H, W, C)), -4.0, 4.0)
    return (base * cell_scale * channel_scale).astype(jnp.float32).astype(jnp.bfloat16)


def table_draw(key):
    base = jnp.clip(jax.random.normal(key, (BUCKETS, HEADS)), -4.0, 4.0)
    return base.astype(jnp.float32)


def draw_blk_table(key, part):
    return table_draw(jax.random.fold_in(key, 5))


def draw_grid_table(key, part):
    return table_draw(jax.random.fold_in(key, 9))


def index_draw(key):
    order = jax.random.permutation(key, BUCKETS)
    position = jnp.arange(64, dtype=jnp.int32)
    prow = position // 8
    pcol = position % 8
    offsets = (prow[:, None] - prow[None, :] + 7) * 15 + (pcol[:, None] - pcol[None, :] + 7)
    return order[offsets].astype(jnp.int32)


def draw_blk_index(key, part):
    return index_draw(jax.random.fold_in(key, 11))


def draw_grid_index(key, part):
    return index_draw(jax.random.fold_in(key, 13))


def centred(key, extent, scale, reach, kind=jnp.bfloat16):
    return jnp.clip(scale * jax.random.normal(key, extent, jnp.float32), -reach, reach).astype(kind)


def setup_inputs(seed: int = 0) -> dict:
    key_list = jax.random.split(jax.random.key(seed), 17)
    field = draw_field(jax.random.fold_in(key_list[16], 71), 0)
    expand_w = centred(key_list[1], (C, EXPAND), C ** -0.5, 0.375)
    dw_kernel = centred(key_list[2], (9, EXPAND), 9 ** -0.5, 2.0, jnp.float32)
    project_w = centred(key_list[3], (EXPAND, C), EXPAND ** -0.5, 0.1875)
    blk_qkv = centred(key_list[4], (C, 3 * C), C ** -0.5, 0.375)
    blk_out = centred(key_list[5], (C, C), C ** -0.5, 0.375)
    blk_table = draw_blk_table(jax.random.fold_in(key_list[16], 71), 0)
    blk_index = draw_blk_index(jax.random.fold_in(key_list[16], 71), 0)
    blk_up = centred(key_list[8], (C, FFN), C ** -0.5, 0.375)
    blk_down = centred(key_list[9], (FFN, C), FFN ** -0.5, 0.1875)
    grid_qkv = centred(key_list[10], (C, 3 * C), C ** -0.5, 0.375)
    grid_out = centred(key_list[11], (C, C), C ** -0.5, 0.375)
    grid_table = draw_grid_table(jax.random.fold_in(key_list[16], 71), 0)
    grid_index = draw_grid_index(jax.random.fold_in(key_list[16], 71), 0)
    grid_up = centred(key_list[14], (C, FFN), C ** -0.5, 0.375)
    grid_down = centred(key_list[15], (FFN, C), FFN ** -0.5, 0.1875)
    return dict(field=field, expand_w=expand_w, dw_kernel=dw_kernel, project_w=project_w, blk_qkv=blk_qkv, blk_out=blk_out, blk_table=blk_table, blk_index=blk_index, blk_up=blk_up, blk_down=blk_down, grid_qkv=grid_qkv, grid_out=grid_out, grid_table=grid_table, grid_index=grid_index, grid_up=grid_up, grid_down=grid_down)


EPS = 1e-05

def normalize(values):
    wide = values.astype(jnp.float32)
    center = wide - lax.optimization_barrier(jnp.mean(wide, axis=-1, keepdims=True))
    spread = lax.optimization_barrier(jnp.mean(center * center, axis=-1, keepdims=True))
    return (center * lax.rsqrt(spread + EPS)).astype(jnp.bfloat16)

def relative(table, index):
    return jnp.transpose(table[index], (2, 0, 1)).astype(jnp.float32)

def feed_forward(values, up_w, down_w):
    inner = jax.nn.gelu(jnp.dot(normalize(values), up_w, preferred_element_type=jnp.float32)).astype(jnp.bfloat16)
    return (values.astype(jnp.float32) + jnp.dot(inner, down_w, preferred_element_type=jnp.float32)).astype(jnp.bfloat16)

def attention_layer(windows, qkv_w, out_w, bias, up_w, down_w):
    nwin = windows.shape[0]
    flat = windows.reshape(nwin * 64, C)
    qkv = jnp.dot(normalize(flat), qkv_w, preferred_element_type=jnp.float32).astype(jnp.bfloat16)
    qkv = qkv.reshape(nwin, 64, 3, HEADS, C // HEADS).astype(jnp.float32)
    scores = jnp.einsum('wphd,wqhd->whpq', qkv[:, :, 0], qkv[:, :, 1])
    scores = scores / math.sqrt(C // HEADS) + bias[None]
    weights = jax.nn.softmax(scores, axis=-1).astype(jnp.bfloat16).astype(jnp.float32)
    mixed = jnp.einsum('whpq,wqhd->wphd', weights, qkv[:, :, 2]).astype(jnp.bfloat16)
    mixed = mixed.reshape(nwin * 64, C)
    current = (flat.astype(jnp.float32) + jnp.dot(mixed, out_w, preferred_element_type=jnp.float32)).astype(jnp.bfloat16)
    return feed_forward(current, up_w, down_w).reshape(nwin, 64, C)

def reference(field, expand_w, dw_kernel, project_w, blk_qkv, blk_out, blk_table, blk_index, blk_up, blk_down, grid_qkv, grid_out, grid_table, grid_index, grid_up, grid_down):
    normed = normalize(field)
    padded = jnp.pad(normed, ((1, 1), (1, 1), (0, 0)))

    def conv_strip(start):
        rows_in = lax.dynamic_slice_in_dim(padded, start, 10, 0)
        hidden = jax.nn.gelu(jnp.dot(rows_in.reshape(-1, C), expand_w, preferred_element_type=jnp.float32))
        hidden = hidden.astype(jnp.bfloat16).reshape(10, W + 2, EXPAND)
        depth = jnp.zeros((8, W, EXPAND), jnp.float32)
        for row_step in range(3):
            for col_step in range(3):
                depth = depth + dw_kernel[3 * row_step + col_step] * hidden[row_step:row_step + 8, col_step:col_step + W].astype(jnp.float32)
        activated = jax.nn.gelu(depth).astype(jnp.bfloat16)
        return jnp.dot(activated.reshape(-1, EXPAND), project_w, preferred_element_type=jnp.float32).reshape(8, W, C)
    starts = (jnp.arange(H // 8) * 8).astype(jnp.int32)
    branch = lax.map(conv_strip, starts).reshape(H, W, C)
    current = (field.astype(jnp.float32) + branch).astype(jnp.bfloat16)
    blk_bias = relative(blk_table, blk_index)

    def block_strip(strip):
        windows = strip.reshape(8, W // 8, 8, C).transpose(1, 0, 2, 3).reshape(-1, 64, C)
        result = attention_layer(windows, blk_qkv, blk_out, blk_bias, blk_up, blk_down)
        return result.reshape(W // 8, 8, 8, C).transpose(1, 0, 2, 3).reshape(8, W, C)
    current = lax.map(block_strip, current.reshape(H // 8, 8, W, C)).reshape(H, W, C)
    grid_bias = relative(grid_table, grid_index)
    grouped = current.reshape(8, H // 8, W, C).transpose(1, 0, 2, 3)

    def grid_slab(slab):
        windows = slab.reshape(8, 8, W // 8, C).transpose(2, 0, 1, 3).reshape(-1, 64, C)
        result = attention_layer(windows, grid_qkv, grid_out, grid_bias, grid_up, grid_down)
        return result.reshape(W // 8, 8, 8, C).transpose(1, 2, 0, 3).reshape(8, W, C)
    result = lax.map(grid_slab, grouped)
    return result.transpose(1, 0, 2, 3).reshape(H, W, C)
```

```python
import functools
import math

import jax
import jax.numpy as jnp
from jax import lax
from jax.experimental import pallas as pl
from jax.experimental.pallas import tpu as pltpu
from jax.sharding import PartitionSpec as P

EPS = 1e-05
HEADS = 8
SIDE = 8
TOKENS = SIDE * SIDE
GROUP = 16
LOG2E = math.log2(math.e)
VMEM_LIMIT = 56 * 1024 * 1024


def halo(field):
    def shifted(x, axis):
        count = lax.axis_size(axis)
        up = [(i, i + 1) for i in range(count - 1)]
        down = [(j, i) for i, j in up]
        return up, down

    up, down = shifted(field, "ha")
    top = lax.ppermute(field[-1:], "ha", up)
    bottom = lax.ppermute(field[:1], "ha", down)
    tall = jnp.concatenate([top, field, bottom], axis=0)
    up, down = shifted(field, "wa")
    left = lax.ppermute(tall[:, -1], "wa", up)
    right = lax.ppermute(tall[:, 0], "wa", down)
    rows, cols, width = tall.shape
    inner = tall.reshape(rows, cols // SIDE, SIDE, width).transpose(0, 2, 1, 3)
    before = jnp.concatenate([left[:, None], inner[:, -1, :-1]], axis=1)
    after = jnp.concatenate([inner[:, 0, 1:], right[:, None]], axis=1)
    return jnp.concatenate([before[:, None], inner, after[:, None]], axis=1)


def norm(wide):
    center = wide - jnp.mean(wide, axis=-1, keepdims=True)
    spread = jnp.mean(center * center, axis=-1, keepdims=True)
    return (center * lax.rsqrt(spread + EPS)).astype(jnp.bfloat16)


def gelu(v):
    kind = v.dtype
    first = jnp.asarray(math.sqrt(2 / math.pi), kind)
    third = jnp.asarray(math.sqrt(2 / math.pi) * 0.044715, kind)
    half = jnp.asarray(0.5, kind) * v
    return half + half * jnp.tanh(v * (first + third * (v * v)))


def put(ref, rows, value):
    for c in range(value.shape[1] // 128):
        ref[c, rows, :] = value[:, c * 128 : (c + 1) * 128]


def get(ref, rows, first=0, last=None):
    last = ref.shape[0] if last is None else last
    return jnp.concatenate([ref[c, rows, :] for c in range(first, last)], axis=1)


def dot(a, b):
    return jnp.dot(a, b, preferred_element_type=jnp.float32)


def attention(x_s, qkv_s, mix_s, qkv_w, bias, mask):
    tiles, cells, lane = x_s.shape
    width = tiles * lane
    block = 256
    scale = LOG2E / math.sqrt(width // HEADS)

    def project(i, _):
        rows = pl.ds(pl.multiple_of(i * block, block), block)
        qkv = dot(norm(get(x_s, rows)), qkv_w[...])
        put(qkv_s, rows, jnp.concatenate([qkv[:, :width] * scale, qkv[:, width:]], axis=1))
        return 0

    lax.fori_loop(0, cells // block, project, 0)
    low = lax.broadcasted_iota(jnp.int32, (TOKENS, 2 * TOKENS), 1) < TOKENS

    def one(w):
        rows = pl.ds(w, TOKENS, stride=GROUP)
        q = get(qkv_s, rows, 0, tiles).astype(jnp.bfloat16)
        k = get(qkv_s, rows, tiles, 2 * tiles).astype(jnp.bfloat16)
        v = get(qkv_s, rows, 2 * tiles).astype(jnp.bfloat16)
        keys = jnp.concatenate([k] * HEADS, axis=0) * mask[...]
        vals = jnp.concatenate([v] * HEADS, axis=0) * mask[...]
        s = lax.dot_general(
            q, keys, (((1,), (1,)), ((), ())), preferred_element_type=jnp.float32
        )
        parts = []
        for c in range(HEADS // 2):
            lanes = slice(c * 2 * TOKENS, (c + 1) * 2 * TOKENS)
            part = s[:, lanes] + bias[:, lanes]
            one_max = jnp.max(jnp.where(low, part, -jnp.inf), axis=1, keepdims=True)
            two_max = jnp.max(jnp.where(low, -jnp.inf, part), axis=1, keepdims=True)
            parts.append(jnp.exp2(part - jnp.where(low, one_max, two_max)).astype(jnp.bfloat16))
        p = jnp.concatenate(parts, axis=1)
        put(mix_s, rows, dot(p, vals) / dot(p, mask[...]))

    for w in range(GROUP):
        one(w)


def feed_forward(x_s, mix_s, out_w, up_w, down_w, store):
    cells = x_s.shape[1]
    block = 256

    def step(i, _):
        rows = pl.ds(pl.multiple_of(i * block, block), block)
        x = get(x_s, rows) + dot(get(mix_s, rows).astype(jnp.bfloat16), out_w[...])
        x = x.astype(jnp.bfloat16).astype(jnp.float32)
        inner = gelu(dot(norm(x), up_w[...]).astype(jnp.bfloat16))
        store(rows, x + dot(inner, down_w[...]))
        return 0

    lax.fori_loop(0, cells // block, step, 0)


def block_kernel(
    field, expand_w, dw, project_w, qkv_w, out_w, bias, up_w, down_w, mask, out,
    hidden, act, x_s, qkv_s, mix_s,
):
    width = field.shape[-1]
    channels = expand_w.shape[-1]
    span = SIDE + 2

    def expand(y, _):
        cells = field[y].reshape(span * GROUP, width).astype(jnp.float32)
        inner = gelu(dot(norm(cells), expand_w[...]).astype(jnp.bfloat16))
        hidden[y] = inner.reshape(span, GROUP, channels)
        return 0

    lax.fori_loop(0, span, expand, 0)

    def depthwise(y, _):
        for b in range(channels // 256):
            lanes = slice(b * 256, (b + 1) * 256)
            total = None
            for dy in range(3):
                for dx in range(3):
                    term = hidden[y + dy, dx : dx + SIDE, :, lanes] * dw[3 * dy + dx, :, lanes][None]
                    total = term if total is None else total + term
            act[:, lanes] = gelu(total).reshape(SIDE * GROUP, 256)
        center = field[y + 1, 1 : 1 + SIDE].reshape(SIDE * GROUP, width).astype(jnp.float32)
        x = center + dot(act[...], project_w[...])
        rows = pl.ds(pl.multiple_of(y * (SIDE * GROUP), SIDE * GROUP), SIDE * GROUP)
        put(x_s, rows, x.astype(jnp.bfloat16).astype(jnp.float32))
        return 0

    lax.fori_loop(0, SIDE, depthwise, 0)
    attention(x_s, qkv_s, mix_s, qkv_w, bias, mask)

    def store(rows, value):
        put(x_s, rows, value)

    feed_forward(x_s, mix_s, out_w, up_w, down_w, store)
    for w in range(GROUP):
        out[w] = get(x_s, pl.ds(w, TOKENS, stride=GROUP)).astype(jnp.bfloat16)


def grid_kernel(
    moved, qkv_w, out_w, bias, up_w, down_w, mask, out, x_s, qkv_s, mix_s
):
    put(x_s, slice(None), moved[...].astype(jnp.float32))
    attention(x_s, qkv_s, mix_s, qkv_w, bias, mask)

    def store(rows, value):
        out[rows, :] = value.astype(jnp.bfloat16)

    feed_forward(x_s, mix_s, out_w, up_w, down_w, store)


def position_bias(table, index):
    buckets = table.shape[0]
    onehot = (index[:, :, None] == lax.broadcasted_iota(jnp.int32, (1, 1, buckets), 2)).astype(
        jnp.float32
    )
    bias = jnp.einsum("pqk,kh->phq", onehot, table * LOG2E, precision=lax.Precision.HIGHEST)
    return bias.reshape(index.shape[0], -1)


def on_device(
    field,
    expand_w,
    dw_kernel,
    project_w,
    blk_qkv,
    blk_out,
    blk_table,
    blk_index,
    blk_up,
    blk_down,
    grid_qkv,
    grid_out,
    grid_table,
    grid_index,
    grid_up,
    grid_down,
):
    rows, cols, width = field.shape
    channels = expand_w.shape[1]
    n_ha = lax.axis_size("ha")
    n_wa = lax.axis_size("wa")
    lead = SIDE // n_ha
    stride_rows = rows // lead
    chunks = rows // (2 * SIDE)
    chunk_rows = stride_rows // chunks
    part_rows = chunk_rows // n_ha
    part_cols = cols // n_wa
    strips = 2
    cells = GROUP * TOKENS

    blk_bias = position_bias(blk_table, blk_index)
    i = jnp.arange(n_ha)[:, None, None] * lead + jnp.arange(lead)[None, None, :]
    j = jnp.arange(SIDE)[None, :, None]
    order = (SIDE * i + j).reshape(-1)
    grid_bias = position_bias(grid_table, grid_index[order][:, order])
    mask = (
        (lax.broadcasted_iota(jnp.int32, (HEADS * TOKENS, width), 0) // TOKENS)
        == (lax.broadcasted_iota(jnp.int32, (HEADS * TOKENS, width), 1) // (width // HEADS))
    ).astype(jnp.bfloat16)
    dw = jnp.broadcast_to(dw_kernel.astype(jnp.bfloat16)[:, None], (9, GROUP, channels))

    framed = halo(field)
    params = pltpu.CompilerParams(vmem_limit_bytes=VMEM_LIMIT)
    scratch = [
        pltpu.VMEM((width // 128, cells, 128), jnp.float32),
        pltpu.VMEM((3 * width // 128, cells, 128), jnp.float32),
        pltpu.VMEM((width // 128, cells, 128), jnp.float32),
    ]
    block = pl.pallas_call(
        block_kernel,
        out_shape=jax.ShapeDtypeStruct((GROUP, TOKENS, width), jnp.bfloat16),
        scratch_shapes=[
            pltpu.VMEM((SIDE + 2, SIDE + 2, GROUP, channels), jnp.bfloat16),
            pltpu.VMEM((SIDE * GROUP, channels), jnp.bfloat16),
        ]
        + scratch,
        compiler_params=params,
        cost_estimate=pl.CostEstimate(
            flops=2 * cells * width * 22 * width, bytes_accessed=4 << 20, transcendentals=0
        ),
    )
    grid = pl.pallas_call(
        grid_kernel,
        out_shape=jax.ShapeDtypeStruct((cells, width), jnp.bfloat16),
        scratch_shapes=scratch,
        compiler_params=params,
        cost_estimate=pl.CostEstimate(
            flops=2 * cells * width * 14 * width, bytes_accessed=3 << 20, transcendentals=0
        ),
    )

    def exchange(x):
        return lax.all_to_all(x, ("ha", "wa"), split_axis=0, concat_axis=0, tiled=True)

    per = cells // (n_ha * n_wa)
    sent = []
    for k in range(chunks):
        starts = [
            (m // (strips // lead)) * stride_rows + k * chunk_rows + (m % (strips // lead)) * SIDE
            for m in range(strips)
        ]
        strip = jnp.stack([framed[s : s + SIDE + 2] for s in starts], axis=2)
        strip = strip.reshape(SIDE + 2, SIDE + 2, GROUP, width)
        done = block(
            strip, expand_w, dw, project_w, blk_qkv, blk_out, blk_bias, blk_up, blk_down, mask
        )
        done = done.reshape(strips, cols // SIDE, SIDE, SIDE, width).transpose(0, 2, 1, 3, 4)
        done = done.reshape(lead, n_ha, part_rows, n_wa, part_cols, width)
        done = done.transpose(1, 3, 0, 2, 4, 5).reshape(n_ha * n_wa, per, width)
        sent.append(exchange(done))
    back = []
    for moved in sent:
        result = grid(
            moved.reshape(cells, width), grid_qkv, grid_out, grid_bias, grid_up, grid_down, mask
        )
        back.append(exchange(result.reshape(n_ha * n_wa, per, width)))
    updated = jnp.stack(back).reshape(chunks, n_ha, n_wa, lead, part_rows, part_cols, width)
    return updated.transpose(3, 0, 1, 4, 2, 5, 6).reshape(rows, cols, width)


def solution(mesh):
    placed = (P("ha", "wa", None),) + (P(),) * 15
    return jax.shard_map(
        on_device, mesh=mesh, in_specs=placed, out_specs=P("ha", "wa", None), check_vma=False
    )
```

```python
import functools
import math

import jax
import jax.numpy as jnp
from jax import lax
from jax.experimental import pallas as pl
from jax.experimental.pallas import tpu as pltpu
from jax.sharding import PartitionSpec as P

EPS = 1e-05
HEADS = 8
SIDE = 8
TOKENS = SIDE * SIDE
GROUP = 16
LOG2E = math.log2(math.e)
MESH = pl.DeviceIdType.MESH
VMEM_LIMIT = 56 * 1024 * 1024


def halo(field):
    def shifted(x, axis):
        count = lax.axis_size(axis)
        up = [(i, i + 1) for i in range(count - 1)]
        down = [(j, i) for i, j in up]
        return up, down

    up, down = shifted(field, "ha")
    top = lax.ppermute(field[-1:], "ha", up)
    bottom = lax.ppermute(field[:1], "ha", down)
    tall = jnp.concatenate([top, field, bottom], axis=0)
    up, down = shifted(field, "wa")
    left = lax.ppermute(tall[:, -1], "wa", up)
    right = lax.ppermute(tall[:, 0], "wa", down)
    rows, cols, width = tall.shape
    inner = tall.reshape(rows, cols // SIDE, SIDE, width).transpose(0, 2, 1, 3)
    before = jnp.concatenate([left[:, None], inner[:, -1, :-1]], axis=1)
    after = jnp.concatenate([inner[:, 0, 1:], right[:, None]], axis=1)
    return jnp.concatenate([before[:, None], inner, after[:, None]], axis=1)


def norm(wide):
    center = wide - jnp.mean(wide, axis=-1, keepdims=True)
    spread = jnp.mean(center * center, axis=-1, keepdims=True)
    return (center * lax.rsqrt(spread + EPS)).astype(jnp.bfloat16)


def gelu(v):
    kind = v.dtype
    first = jnp.asarray(math.sqrt(2 / math.pi), kind)
    third = jnp.asarray(math.sqrt(2 / math.pi) * 0.044715, kind)
    half = jnp.asarray(0.5, kind) * v
    return half + half * jnp.tanh(v * (first + third * (v * v)))


def put(ref, rows, value):
    for c in range(value.shape[1] // 128):
        ref[c, rows, :] = value[:, c * 128 : (c + 1) * 128]


def get(ref, rows, first=0, last=None):
    last = ref.shape[0] if last is None else last
    return jnp.concatenate([ref[c, rows, :] for c in range(first, last)], axis=1)


def dot(a, b):
    return jnp.dot(a, b, preferred_element_type=jnp.float32)


def attention(x_s, qkv_s, mix_s, qkv_w, bias, mask):
    tiles, cells, lane = x_s.shape
    width = tiles * lane
    block = 256
    scale = LOG2E / math.sqrt(width // HEADS)

    def project(i, _):
        rows = pl.ds(pl.multiple_of(i * block, block), block)
        qkv = dot(norm(get(x_s, rows)), qkv_w[...])
        put(qkv_s, rows, jnp.concatenate([qkv[:, :width] * scale, qkv[:, width:]], axis=1))
        return 0

    lax.fori_loop(0, cells // block, project, 0)
    low = lax.broadcasted_iota(jnp.int32, (TOKENS, 2 * TOKENS), 1) < TOKENS

    def one(w):
        rows = pl.ds(w, TOKENS, stride=GROUP)
        q = get(qkv_s, rows, 0, tiles).astype(jnp.bfloat16)
        k = get(qkv_s, rows, tiles, 2 * tiles).astype(jnp.bfloat16)
        v = get(qkv_s, rows, 2 * tiles).astype(jnp.bfloat16)
        keys = jnp.concatenate([k] * HEADS, axis=0) * mask[...]
        vals = jnp.concatenate([v] * HEADS, axis=0) * mask[...]
        s = lax.dot_general(
            q, keys, (((1,), (1,)), ((), ())), preferred_element_type=jnp.float32
        )
        parts = []
        for c in range(HEADS // 2):
            lanes = slice(c * 2 * TOKENS, (c + 1) * 2 * TOKENS)
            part = s[:, lanes] + bias[:, lanes]
            one_max = jnp.max(jnp.where(low, part, -jnp.inf), axis=1, keepdims=True)
            two_max = jnp.max(jnp.where(low, -jnp.inf, part), axis=1, keepdims=True)
            parts.append(jnp.exp2(part - jnp.where(low, one_max, two_max)).astype(jnp.bfloat16))
        p = jnp.concatenate(parts, axis=1)
        put(mix_s, rows, dot(p, vals) / dot(p, mask[...]))

    def several(g, _):
        for w in range(4):
            one(g * 4 + w)
        return 0

    lax.fori_loop(0, GROUP // 4, several, 0)


def feed_forward(i, block, x_s, mix_s, out_w, up_w, down_w):
    rows = pl.ds(pl.multiple_of(i * block, block), block)
    x = get(x_s, rows) + dot(get(mix_s, rows).astype(jnp.bfloat16), out_w[...])
    x = x.astype(jnp.bfloat16).astype(jnp.float32)
    inner = gelu(dot(norm(x), up_w[...]).astype(jnp.bfloat16))
    return rows, x + dot(inner, down_w[...])


def convolve(k, field, expand_w, dw, project_w, hidden, act, x_s):
    width = field.shape[-1]
    channels = expand_w.shape[-1]
    span = SIDE + 2

    def expand(y, _):
        cells = field[k, y].reshape(span * GROUP, width).astype(jnp.float32)
        inner = gelu(dot(norm(cells), expand_w[...]).astype(jnp.bfloat16))
        hidden[y] = inner.reshape(span, GROUP, channels)
        return 0

    lax.fori_loop(0, span, expand, 0)

    def depthwise(y, _):
        for b in range(channels // 256):
            lanes = slice(b * 256, (b + 1) * 256)
            total = None
            for dy in range(3):
                for dx in range(3):
                    term = hidden[y + dy, dx : dx + SIDE, :, lanes] * dw[3 * dy + dx, :, lanes][None]
                    total = term if total is None else total + term
            act[:, lanes] = gelu(total).reshape(SIDE * GROUP, 256)
        center = field[k, y + 1, 1 : 1 + SIDE].reshape(SIDE * GROUP, width).astype(jnp.float32)
        x = center + dot(act[...], project_w[...])
        rows = pl.ds(pl.multiple_of(y * (SIDE * GROUP), SIDE * GROUP), SIDE * GROUP)
        put(x_s, rows, x.astype(jnp.bfloat16).astype(jnp.float32))
        return 0

    lax.fori_loop(0, SIDE, depthwise, 0)


def layer_kernel(
    lead, n_ha, n_wa, part_rows, part_cols,
    field, expand_w, dw, project_w, blk_qkv, blk_out, blk_bias, blk_up, blk_down,
    grid_qkv, grid_out, grid_bias, grid_up, grid_down, mask,
    out,
    hidden, act, x_s, qkv_s, mix_s, ready, arrived, result,
    send_go, recv_go, send_back, recv_back,
):
    chunks, devices, per, width = out.shape
    my_ha, my_wa = lax.axis_index("ha"), lax.axis_index("wa")
    me = my_ha * n_wa + my_wa
    blocks = SIDE // part_rows
    size = part_rows * SIDE * GROUP
    share = devices // blocks
    lines = part_rows * part_cols

    barrier = pltpu.get_barrier_semaphore()

    def greet(o, _):
        d = lax.rem(me + o, devices)
        pl.semaphore_signal(
            barrier, inc=1, device_id=(d // n_wa, lax.rem(d, n_wa)), device_id_type=MESH
        )
        return 0

    lax.fori_loop(1, devices, greet, 0)

    def ship(k, d, source, target, send_sem, recv_sem):
        @pl.when(d != me)
        def _():
            pltpu.make_async_remote_copy(
                src_ref=source.at[k, d],
                dst_ref=target.at[k, me],
                send_sem=send_sem.at[k],
                recv_sem=recv_sem.at[k],
                device_id=(d // n_wa, lax.rem(d, n_wa)),
                device_id_type=MESH,
            ).start()

        @pl.when(d == me)
        def _():
            target[k, d] = source[k, d]

    def all_of(k, source, target, send_sem, recv_sem):
        other = lax.rem(me + 1, devices)
        return pltpu.make_async_remote_copy(
            src_ref=source.at[k, pl.ds(0, devices - 1)],
            dst_ref=target.at[k, pl.ds(0, devices - 1)],
            send_sem=send_sem.at[k],
            recv_sem=recv_sem.at[k],
            device_id=(other // n_wa, lax.rem(other, n_wa)),
            device_id_type=MESH,
        )

    def block_chunk(k, _):
        convolve(k, field, expand_w, dw, project_w, hidden, act, x_s)
        attention(x_s, qkv_s, mix_s, blk_qkv, blk_bias, mask)

        @pl.when(k == 0)
        def _():
            pl.semaphore_wait(barrier, devices - 1)

        def step(n, _):
            i = lax.rem(n + my_ha + 1, blocks)
            rows, value = feed_forward(i, size, x_s, mix_s, blk_out, blk_up, blk_down)
            put(x_s, rows, value)
            for w in range(GROUP):
                strip, square = w // SIDE, w % SIDE
                for h in range(SIDE // part_cols):
                    first = h * part_cols * GROUP + w
                    piece = jnp.concatenate(
                        [
                            get(
                                x_s,
                                pl.ds(
                                    i * size + r * SIDE * GROUP + first, part_cols, stride=GROUP
                                ),
                            )
                            for r in range(part_rows)
                        ],
                        axis=0,
                    ).astype(jnp.bfloat16)
                    if lead == 2:
                        ready[k, i * n_wa + square, strip * lines : (strip + 1) * lines] = piece
                    else:
                        row = strip * blocks + i
                        ready[k, row * n_wa + square * (SIDE // part_cols) + h] = piece

            def go(o, _):
                d = lax.rem(my_wa + o, n_wa)
                for strip in range(2 // lead):
                    ship(
                        k, (strip * blocks + i) * n_wa + d, ready, arrived, send_go, recv_go
                    )
                return 0

            lax.fori_loop(0, n_wa, go, 0)
            return 0

        lax.fori_loop(0, blocks, step, 0)
        return 0

    lax.fori_loop(0, chunks, block_chunk, 0)

    def grid_chunk(k, _):
        all_of(k, ready, arrived, send_go, recv_go).wait_recv()
        put(x_s, slice(None), arrived[k].astype(jnp.float32).reshape(devices * per, width))
        attention(x_s, qkv_s, mix_s, grid_qkv, grid_bias, mask)

        def step(n, _):
            i = lax.rem(n + my_ha + 1, blocks)
            rows, value = feed_forward(i, size, x_s, mix_s, grid_out, grid_up, grid_down)
            first = pl.multiple_of(i * share, share)
            result[k, pl.ds(first, share)] = value.reshape(share, per, width).astype(jnp.bfloat16)

            def go(o, _):
                d = i * share + lax.rem(my_wa + o, share)
                ship(k, d, result, out, send_back, recv_back)
                return 0

            lax.fori_loop(0, share, go, 0)
            return 0

        lax.fori_loop(0, blocks, step, 0)
        return 0

    lax.fori_loop(0, chunks, grid_chunk, 0)

    def finish(k, _):
        all_of(k, ready, arrived, send_go, recv_go).wait_send()
        all_of(k, result, out, send_back, recv_back).wait()
        return 0

    lax.fori_loop(0, chunks, finish, 0)


def position_bias(table, index):
    buckets = table.shape[0]
    onehot = (index[:, :, None] == lax.broadcasted_iota(jnp.int32, (1, 1, buckets), 2)).astype(
        jnp.float32
    )
    bias = jnp.einsum("pqk,kh->phq", onehot, table * LOG2E, precision=lax.Precision.HIGHEST)
    return bias.reshape(index.shape[0], -1)


def on_device(
    field,
    expand_w,
    dw_kernel,
    project_w,
    blk_qkv,
    blk_out,
    blk_table,
    blk_index,
    blk_up,
    blk_down,
    grid_qkv,
    grid_out,
    grid_table,
    grid_index,
    grid_up,
    grid_down,
):
    rows, cols, width = field.shape
    channels = expand_w.shape[1]
    n_ha = lax.axis_size("ha")
    n_wa = lax.axis_size("wa")
    lead = SIDE // n_ha
    stride_rows = rows // lead
    chunks = rows // (2 * SIDE)
    chunk_rows = stride_rows // chunks
    part_rows = chunk_rows // n_ha
    part_cols = cols // n_wa
    strips = 2
    cells = GROUP * TOKENS

    blk_bias = position_bias(blk_table, blk_index)
    i = jnp.arange(n_ha)[:, None, None] * lead + jnp.arange(lead)[None, None, :]
    j = jnp.arange(SIDE)[None, :, None]
    order = (SIDE * i + j).reshape(-1)
    grid_bias = position_bias(grid_table, grid_index[order][:, order])
    mask = (
        (lax.broadcasted_iota(jnp.int32, (HEADS * TOKENS, width), 0) // TOKENS)
        == (lax.broadcasted_iota(jnp.int32, (HEADS * TOKENS, width), 1) // (width // HEADS))
    ).astype(jnp.bfloat16)
    dw = jnp.broadcast_to(dw_kernel.astype(jnp.bfloat16)[:, None], (9, GROUP, channels))

    framed = halo(field)
    per = cells // (n_ha * n_wa)
    starts = [
        (m // (strips // lead)) * stride_rows + (m % (strips // lead)) * SIDE
        for m in range(strips)
    ]
    strip = jnp.stack(
        [
            jnp.stack([framed[s + k * chunk_rows :][: SIDE + 2] for s in starts], axis=2)
            for k in range(chunks)
        ]
    ).reshape(chunks, SIDE + 2, SIDE + 2, GROUP, width)
    parts = (chunks, n_ha * n_wa, per, width)
    layer = pl.pallas_call(
        functools.partial(layer_kernel, lead, n_ha, n_wa, part_rows, part_cols),
        out_shape=jax.ShapeDtypeStruct(parts, jnp.bfloat16),
        in_specs=[pl.BlockSpec(memory_space=pltpu.VMEM)] * 15,
        out_specs=pl.BlockSpec(memory_space=pltpu.VMEM),
        scratch_shapes=[
            pltpu.VMEM((SIDE + 2, SIDE + 2, GROUP, channels), jnp.bfloat16),
            pltpu.VMEM((SIDE * GROUP, channels), jnp.bfloat16),
            pltpu.VMEM((width // 128, cells, 128), jnp.float32),
            pltpu.VMEM((3 * width // 128, cells, 128), jnp.float32),
            pltpu.VMEM((width // 128, cells, 128), jnp.float32),
            pltpu.VMEM(parts, jnp.bfloat16),
            pltpu.VMEM(parts, jnp.bfloat16),
            pltpu.VMEM(parts, jnp.bfloat16),
        ]
        + [pltpu.SemaphoreType.DMA((chunks,))] * 4,
        compiler_params=pltpu.CompilerParams(
            vmem_limit_bytes=VMEM_LIMIT, collective_id=0, has_side_effects=True
        ),
        cost_estimate=pl.CostEstimate(
            flops=2 * rows * cols * width * 36 * width, bytes_accessed=12 << 20, transcendentals=0
        ),
    )
    back = layer(
        strip, expand_w, dw, project_w, blk_qkv, blk_out, blk_bias, blk_up, blk_down,
        grid_qkv, grid_out, grid_bias, grid_up, grid_down, mask,
    )
    updated = back.reshape(chunks, n_ha, n_wa, lead, part_rows, part_cols, width)
    return updated.transpose(3, 0, 1, 4, 2, 5, 6).reshape(rows, cols, width)


def solution(mesh):
    placed = (P("ha", "wa", None),) + (P(),) * 15
    return jax.shard_map(
        on_device, mesh=mesh, in_specs=placed, out_specs=P("ha", "wa", None), check_vma=False
    )
```

```python
import functools
import math

import jax
import jax.numpy as jnp
from jax import lax
from jax.experimental import pallas as pl
from jax.experimental.pallas import tpu as pltpu
from jax.sharding import PartitionSpec as P

EPS = 1e-05
HEADS = 8
SIDE = 8
TOKENS = SIDE * SIDE
GROUP = 16
LOG2E = math.log2(math.e)
MESH = pl.DeviceIdType.MESH
VMEM_LIMIT = 56 * 1024 * 1024


def norm(wide):
    center = wide - jnp.mean(wide, axis=-1, keepdims=True)
    spread = jnp.mean(center * center, axis=-1, keepdims=True)
    return (center * lax.rsqrt(spread + EPS)).astype(jnp.bfloat16)


def gelu(v):
    kind = v.dtype
    first = jnp.asarray(math.sqrt(2 / math.pi), kind)
    third = jnp.asarray(math.sqrt(2 / math.pi) * 0.044715, kind)
    half = jnp.asarray(0.5, kind) * v
    return half + half * jnp.tanh(v * (first + third * (v * v)))


def put(ref, rows, value):
    for c in range(value.shape[1] // 128):
        ref[c, rows, :] = value[:, c * 128 : (c + 1) * 128]


def get(ref, rows, first=0, last=None):
    last = ref.shape[0] if last is None else last
    return jnp.concatenate([ref[c, rows, :] for c in range(first, last)], axis=1)


def dot(a, b):
    return jnp.dot(a, b, preferred_element_type=jnp.float32)


def attention(x_s, qkv_s, mix_s, qkv_w, bias, mask):
    tiles, cells, lane = x_s.shape
    width = tiles * lane
    block = 512
    scale = LOG2E / math.sqrt(width // HEADS)

    def project(i, _):
        rows = pl.ds(pl.multiple_of(i * block, block), block)
        qkv = dot(norm(get(x_s, rows)), qkv_w[...])
        put(qkv_s, rows, jnp.concatenate([qkv[:, :width] * scale, qkv[:, width:]], axis=1))
        return 0

    lax.fori_loop(0, cells // block, project, 0)
    low = lax.broadcasted_iota(jnp.int32, (TOKENS, 2 * TOKENS), 1) < TOKENS
    several = HEADS // tiles

    def one(w, g):
        rows = pl.ds(w, TOKENS, stride=GROUP)
        q = qkv_s[g, rows, :].astype(jnp.bfloat16)
        k = qkv_s[tiles + g, rows, :].astype(jnp.bfloat16)
        v = qkv_s[2 * tiles + g, rows, :].astype(jnp.bfloat16)
        keys = jnp.concatenate([k] * several, axis=0) * mask[...]
        vals = jnp.concatenate([v] * several, axis=0) * mask[...]
        s = lax.dot_general(
            q, keys, (((1,), (1,)), ((), ())), preferred_element_type=jnp.float32
        )
        parts = []
        for c in range(several // 2):
            lanes = slice(c * 2 * TOKENS, (c + 1) * 2 * TOKENS)
            start = (g * several // 2 + c) * 2 * TOKENS
            part = s[:, lanes] + bias[:, start : start + 2 * TOKENS]
            one_max = jnp.max(jnp.where(low, part, -jnp.inf), axis=1, keepdims=True)
            two_max = jnp.max(jnp.where(low, -jnp.inf, part), axis=1, keepdims=True)
            parts.append(jnp.exp2(part - jnp.where(low, one_max, two_max)).astype(jnp.bfloat16))
        p = jnp.concatenate(parts, axis=1)
        both = dot(p, jnp.concatenate([vals, mask[...]], axis=1))
        mix_s[g, rows, :] = both[:, :lane] / both[:, lane:]

    def step(n, _):
        for w in range(4):
            for g in range(tiles):
                one(n * 4 + w, g)
        return 0

    lax.fori_loop(0, GROUP // 4, step, 0)


def feed_forward(i, block, x_s, mix_s, out_w, up_w, down_w):
    rows = pl.ds(pl.multiple_of(i * block, block), block)
    x = get(x_s, rows) + dot(get(mix_s, rows).astype(jnp.bfloat16), out_w[...])
    x = x.astype(jnp.bfloat16).astype(jnp.float32)
    inner = gelu(dot(norm(x), up_w[...]).astype(jnp.bfloat16))
    return rows, x + dot(inner, down_w[...])


def neighbours():
    return [(dy, dx) for dy in (-1, 0, 1) for dx in (-1, 0, 1) if dy or dx]


def borders(n_ha, n_wa, field, stage, edge, rows_in, cols_in, corners_in, send_sem, recv_sem):
    rows, cols, _ = field.shape
    my_ha, my_wa = lax.axis_index("ha"), lax.axis_index("wa")
    result = []
    for n, (dy, dx) in enumerate(neighbours()):
        there = (my_ha + dy, my_wa + dx)
        exists = (there[0] >= 0) & (there[0] < n_ha) & (there[1] >= 0) & (there[1] < n_wa)
        from_ha, from_wa = my_ha - dy, my_wa - dx
        comes = (from_ha >= 0) & (from_ha < n_ha) & (from_wa >= 0) & (from_wa < n_wa)
        row = 0 if dy < 0 else rows - 1
        low, left = int(dy < 0), int(dx < 0)
        if dx == 0:
            source, target = field.at[row], rows_in.at[low]
        elif dy == 0:
            source, target = edge.at[1 - left], cols_in.at[left]
        else:
            first = 0 if dx < 0 else cols - GROUP
            source, target = field.at[row, pl.ds(first, GROUP)], corners_in.at[2 * low + left]
        copy = pltpu.make_async_remote_copy(
            src_ref=source,
            dst_ref=target,
            send_sem=send_sem.at[n],
            recv_sem=recv_sem.at[n],
            device_id=there,
            device_id_type=MESH,
        )
        result.append((copy, exists, comes, target))
    return result


def convolve(k, starts, chunk_rows, pitch, stage, expand_w, dw, project_w, hidden, act, x_s):
    channels = expand_w.shape[-1]
    span = SIDE + 2

    def row(y, first, last):
        pieces = []
        for t in range(first, last):
            for start in starts:
                at = (start + k * chunk_rows + y) * pitch + SIDE - 1 + t
                pieces.append(get(stage, pl.ds(at, SIDE, stride=SIDE)))
        return pieces

    def expand(n, _):
        cells = jnp.concatenate(row(2 * n, 0, span) + row(2 * n + 1, 0, span), axis=0)
        inner = gelu(dot(norm(cells), expand_w[...]).astype(jnp.bfloat16))
        hidden[pl.ds(2 * n, 2)] = inner.reshape(2, span, GROUP, channels)
        return 0

    lax.fori_loop(0, span // 2, expand, 0)
    size = SIDE * GROUP

    def depthwise(n, _):
        for half in range(2):
            y = 2 * n + half
            for b in range(channels // 256):
                lanes = slice(b * 256, (b + 1) * 256)
                total = None
                for dy in range(3):
                    for dx in range(3):
                        term = (
                            hidden[y + dy, dx : dx + SIDE, :, lanes]
                            * dw[3 * dy + dx, :, lanes][None]
                        )
                        total = term if total is None else total + term
                act[half * size : (half + 1) * size, lanes] = gelu(total).reshape(size, 256)
        center = jnp.concatenate(
            row(2 * n + 1, 1, 1 + SIDE) + row(2 * n + 2, 1, 1 + SIDE), axis=0
        )
        x = center + dot(act[...], project_w[...])
        rows = pl.ds(pl.multiple_of(n * (2 * size), 2 * size), 2 * size)
        put(x_s, rows, x.astype(jnp.bfloat16).astype(jnp.float32))
        return 0

    lax.fori_loop(0, SIDE // 2, depthwise, 0)


def layer_kernel(
    lead, n_ha, n_wa, part_rows, part_cols, starts, chunk_rows,
    field, expand_w, dw_kernel, project_w, blk_qkv, blk_out, blk_bias, blk_up, blk_down,
    grid_qkv, grid_out, grid_bias, grid_up, grid_down,
    out,
    stage, edge, rows_in, cols_in, corners_in, mask, dw, edge_send, edge_recv,
    hidden, act, x_s, qkv_s, mix_s, ready, arrived, result,
    send_go, recv_go, send_back, recv_back,
):
    chunks, devices, per, width = out.shape
    my_ha, my_wa = lax.axis_index("ha"), lax.axis_index("wa")
    me = my_ha * n_wa + my_wa
    blocks = SIDE // part_rows
    size = part_rows * SIDE * GROUP
    share = devices // blocks
    lines = part_rows * part_cols

    barrier = pltpu.get_barrier_semaphore()

    def greet(o, _):
        d = lax.rem(me + o, devices)
        pl.semaphore_signal(
            barrier, inc=1, device_id=(d // n_wa, lax.rem(d, n_wa)), device_id_type=MESH
        )
        return 0

    lax.fori_loop(1, devices, greet, 0)

    rows, cols, _ = field.shape
    pitch = cols + 2 * SIDE

    def lay(y, _):
        at = pl.ds(pl.multiple_of((y + 1) * pitch + SIDE, SIDE), cols)
        put(stage, at, field[y].astype(jnp.float32))
        return 0

    lax.fori_loop(0, rows, lay, 0)
    edge[0] = get(stage, pl.ds(pitch + SIDE, rows, stride=pitch)).astype(jnp.bfloat16)
    edge[1] = get(stage, pl.ds(pitch + SIDE + cols - 1, rows, stride=pitch)).astype(jnp.bfloat16)
    pl.semaphore_wait(barrier, devices - 1)
    crossings = borders(
        n_ha, n_wa, field, stage, edge, rows_in, cols_in, corners_in, edge_send, edge_recv
    )
    for copy, exists, _, _ in crossings:
        pl.when(exists)(copy.start)
    mask[...] = (
        (lax.broadcasted_iota(jnp.int32, mask.shape, 0) // TOKENS)
        == (lax.broadcasted_iota(jnp.int32, mask.shape, 1) // (width // HEADS))
    ).astype(jnp.float32).astype(jnp.bfloat16)
    for tap in range(9):
        dw[tap] = jnp.broadcast_to(dw_kernel[tap : tap + 1, :], dw.shape[1:]).astype(jnp.bfloat16)
    for copy, exists, comes, target in crossings:
        @pl.when(jnp.logical_not(comes))
        def _():
            target[...] = jnp.zeros(target.shape, jnp.bfloat16)

        pl.when(comes)(copy.wait_recv)
        pl.when(exists)(copy.wait_send)
    bottom = (rows + 1) * pitch
    put(stage, slice(SIDE, SIDE + cols), rows_in[0].astype(jnp.float32))
    put(stage, slice(bottom + SIDE, bottom + SIDE + cols), rows_in[1].astype(jnp.float32))
    left, right = SIDE - 1, SIDE + cols
    put(stage, pl.ds(pitch + left, rows, stride=pitch), cols_in[0].astype(jnp.float32))
    put(stage, pl.ds(pitch + right, rows, stride=pitch), cols_in[1].astype(jnp.float32))
    for n, (at, line) in enumerate(
        [(left, GROUP - 1), (right, 0), (bottom + left, GROUP - 1), (bottom + right, 0)]
    ):
        cell = corners_in[n].astype(jnp.float32)[line : line + 1]
        put(stage, slice(at, at + 1), cell)

    def ship(k, d, source, target, send_sem, recv_sem):
        @pl.when(d != me)
        def _():
            pltpu.make_async_remote_copy(
                src_ref=source.at[k, d],
                dst_ref=target.at[k, me],
                send_sem=send_sem.at[k],
                recv_sem=recv_sem.at[k],
                device_id=(d // n_wa, lax.rem(d, n_wa)),
                device_id_type=MESH,
            ).start()

        @pl.when(d == me)
        def _():
            target[k, d] = source[k, d]

    def all_of(k, source, target, send_sem, recv_sem):
        other = lax.rem(me + 1, devices)
        return pltpu.make_async_remote_copy(
            src_ref=source.at[k, pl.ds(0, devices - 1)],
            dst_ref=target.at[k, pl.ds(0, devices - 1)],
            send_sem=send_sem.at[k],
            recv_sem=recv_sem.at[k],
            device_id=(other // n_wa, lax.rem(other, n_wa)),
            device_id_type=MESH,
        )

    def block_chunk(k, _):
        convolve(
            k, starts, chunk_rows, pitch, stage, expand_w, dw, project_w, hidden, act, x_s
        )
        attention(x_s, qkv_s, mix_s, blk_qkv, blk_bias, mask)

        def step(n, _):
            i = lax.rem(n + my_ha + 1, blocks)
            rows, value = feed_forward(i, size, x_s, mix_s, blk_out, blk_up, blk_down)
            put(x_s, rows, value)
            for w in range(GROUP):
                strip, square = w // SIDE, w % SIDE
                for h in range(SIDE // part_cols):
                    first = h * part_cols * GROUP + w
                    piece = jnp.concatenate(
                        [
                            get(
                                x_s,
                                pl.ds(
                                    i * size + r * SIDE * GROUP + first, part_cols, stride=GROUP
                                ),
                            )
                            for r in range(part_rows)
                        ],
                        axis=0,
                    ).astype(jnp.bfloat16)
                    if lead == 2:
                        ready[k, i * n_wa + square, strip * lines : (strip + 1) * lines] = piece
                    else:
                        row = strip * blocks + i
                        ready[k, row * n_wa + square * (SIDE // part_cols) + h] = piece

            def go(o, _):
                d = lax.rem(my_wa + o, n_wa)
                for strip in range(2 // lead):
                    ship(
                        k, (strip * blocks + i) * n_wa + d, ready, arrived, send_go, recv_go
                    )
                return 0

            lax.fori_loop(0, n_wa, go, 0)
            return 0

        lax.fori_loop(0, blocks, step, 0)
        return 0

    lax.fori_loop(0, chunks, block_chunk, 0)

    def grid_chunk(k, _):
        all_of(k, ready, arrived, send_go, recv_go).wait_recv()
        put(x_s, slice(None), arrived[k].astype(jnp.float32).reshape(devices * per, width))
        attention(x_s, qkv_s, mix_s, grid_qkv, grid_bias, mask)

        def step(n, _):
            i = lax.rem(n + my_ha + 1, blocks)
            rows, value = feed_forward(i, size, x_s, mix_s, grid_out, grid_up, grid_down)
            first = pl.multiple_of(i * share, share)
            result[k, pl.ds(first, share)] = value.reshape(share, per, width).astype(jnp.bfloat16)

            def go(o, _):
                d = i * share + lax.rem(my_wa + o, share)
                ship(k, d, result, out, send_back, recv_back)
                return 0

            lax.fori_loop(0, share, go, 0)
            return 0

        lax.fori_loop(0, blocks, step, 0)
        return 0

    lax.fori_loop(0, chunks, grid_chunk, 0)

    def finish(k, _):
        all_of(k, ready, arrived, send_go, recv_go).wait_send()
        all_of(k, result, out, send_back, recv_back).wait()
        return 0

    lax.fori_loop(0, chunks, finish, 0)


def bias_kernel(tables, indices, *outs):
    low = lax.broadcasted_iota(jnp.int32, (TOKENS, 2 * TOKENS), 1) < TOKENS
    for a in range(2):
        index = jnp.concatenate([indices[a], indices[a]], axis=1)
        within = index % 128
        upper = index >= 128
        found = []
        for h in range(HEADS):
            halves = [
                jnp.take_along_axis(
                    jnp.broadcast_to(tables[a, h : h + 1, n * 128 : (n + 1) * 128], index.shape),
                    within,
                    axis=1,
                    mode="promise_in_bounds",
                )
                for n in range(2)
            ]
            found.append(jnp.where(upper, halves[1], halves[0]))
        for c in range(HEADS // 2):
            outs[a][:, c * 2 * TOKENS : (c + 1) * 2 * TOKENS] = (
                jnp.where(low, found[2 * c], found[2 * c + 1]) * LOG2E
            )


def on_device(
    field,
    expand_w,
    dw_kernel,
    project_w,
    blk_qkv,
    blk_out,
    blk_table,
    blk_index,
    blk_up,
    blk_down,
    grid_qkv,
    grid_out,
    grid_table,
    grid_index,
    grid_up,
    grid_down,
):
    rows, cols, width = field.shape
    channels = expand_w.shape[1]
    n_ha = lax.axis_size("ha")
    n_wa = lax.axis_size("wa")
    lead = SIDE // n_ha
    stride_rows = rows // lead
    chunks = rows // (2 * SIDE)
    chunk_rows = stride_rows // chunks
    part_rows = chunk_rows // n_ha
    part_cols = cols // n_wa
    strips = 2
    cells = GROUP * TOKENS

    ordered = grid_index.reshape(n_ha, lead, SIDE, n_ha, lead, SIDE).transpose(0, 2, 1, 3, 5, 4)
    indices = jnp.stack([blk_index, ordered.reshape(TOKENS, TOKENS)])
    tables = jnp.stack([blk_table, grid_table]).transpose(0, 2, 1)
    tables = jnp.pad(tables, ((0, 0), (0, 0), (0, 256 - tables.shape[2])))
    bias = pl.pallas_call(
        bias_kernel,
        out_shape=[jax.ShapeDtypeStruct((TOKENS, HEADS * TOKENS), jnp.float32)] * 2,
    )(tables, indices)
    per = cells // (n_ha * n_wa)
    starts = [
        (m // (strips // lead)) * stride_rows + (m % (strips // lead)) * SIDE
        for m in range(strips)
    ]
    pitch = cols + 2 * SIDE
    parts = (chunks, n_ha * n_wa, per, width)
    layer = pl.pallas_call(
        functools.partial(
            layer_kernel, lead, n_ha, n_wa, part_rows, part_cols, starts, chunk_rows
        ),
        out_shape=jax.ShapeDtypeStruct(parts, jnp.bfloat16),
        in_specs=[pl.BlockSpec(memory_space=pltpu.VMEM)] * 14,
        out_specs=pl.BlockSpec(memory_space=pltpu.VMEM),
        scratch_shapes=[
            pltpu.VMEM((width // 128, (rows + 2) * pitch, 128), jnp.float32),
            pltpu.VMEM((2, rows, width), jnp.bfloat16),
            pltpu.VMEM((2, cols, width), jnp.bfloat16),
            pltpu.VMEM((2, rows, width), jnp.bfloat16),
            pltpu.VMEM((4, GROUP, width), jnp.bfloat16),
            pltpu.VMEM((HEADS * TOKENS * 128 // width, 128), jnp.bfloat16),
            pltpu.VMEM((9, GROUP, channels), jnp.bfloat16),
            pltpu.SemaphoreType.DMA((8,)),
            pltpu.SemaphoreType.DMA((8,)),
            pltpu.VMEM((SIDE + 2, SIDE + 2, GROUP, channels), jnp.bfloat16),
            pltpu.VMEM((2 * SIDE * GROUP, channels), jnp.bfloat16),
            pltpu.VMEM((width // 128, cells, 128), jnp.float32),
            pltpu.VMEM((3 * width // 128, cells, 128), jnp.float32),
            pltpu.VMEM((width // 128, cells, 128), jnp.float32),
            pltpu.VMEM(parts, jnp.bfloat16),
            pltpu.VMEM(parts, jnp.bfloat16),
            pltpu.VMEM(parts, jnp.bfloat16),
        ]
        + [pltpu.SemaphoreType.DMA((chunks,))] * 4,
        compiler_params=pltpu.CompilerParams(
            vmem_limit_bytes=VMEM_LIMIT, collective_id=0, has_side_effects=True
        ),
        cost_estimate=pl.CostEstimate(
            flops=2 * rows * cols * width * 36 * width, bytes_accessed=12 << 20, transcendentals=0
        ),
    )
    back = layer(
        field, expand_w, dw_kernel, project_w, blk_qkv, blk_out, bias[0], blk_up, blk_down,
        grid_qkv, grid_out, bias[1], grid_up, grid_down,
    )
    updated = back.reshape(chunks, n_ha, n_wa, lead, part_rows, part_cols, width)
    return updated.transpose(3, 0, 1, 4, 2, 5, 6).reshape(rows, cols, width)


def solution(mesh):
    placed = (P("ha", "wa", None),) + (P(),) * 15
    return jax.shard_map(
        on_device, mesh=mesh, in_specs=placed, out_specs=P("ha", "wa", None), check_vma=False
    )
```

```python
import functools
import math

import jax
import jax.numpy as jnp
from jax import lax
from jax.experimental import pallas as pl
from jax.experimental.pallas import tpu as pltpu
from jax.sharding import PartitionSpec as P

EPS = 1e-05
HEADS = 8
SIDE = 8
TOKENS = SIDE * SIDE
GROUP = 16
LOG2E = math.log2(math.e)
MESH = pl.DeviceIdType.MESH
VMEM_LIMIT = 56 * 1024 * 1024


def norm(wide):
    center = wide - jnp.mean(wide, axis=-1, keepdims=True)
    spread = jnp.mean(center * center, axis=-1, keepdims=True)
    return (center * lax.rsqrt(spread + EPS)).astype(jnp.bfloat16)


def gelu(v):
    kind = v.dtype
    first = jnp.asarray(math.sqrt(2 / math.pi), kind)
    third = jnp.asarray(math.sqrt(2 / math.pi) * 0.044715, kind)
    half = jnp.asarray(0.5, kind) * v
    return half + half * jnp.tanh(v * (first + third * (v * v)))


def put(ref, rows, value):
    for c in range(value.shape[1] // 128):
        ref[c, rows, :] = value[:, c * 128 : (c + 1) * 128]


def get(ref, rows, first=0, last=None):
    last = ref.shape[0] if last is None else last
    return jnp.concatenate([ref[c, rows, :] for c in range(first, last)], axis=1)


def dot(a, b):
    return jnp.dot(a, b, preferred_element_type=jnp.float32)


def attention(x_s, qkv_s, mix_s, qkv_w, bias, mask):
    tiles, cells, lane = x_s.shape
    width = tiles * lane
    block = 512
    scale = LOG2E / math.sqrt(width // HEADS)

    def project(i, _):
        rows = pl.ds(pl.multiple_of(i * block, block), block)
        qkv = dot(norm(get(x_s, rows)), qkv_w[...])
        put(qkv_s, rows, jnp.concatenate([qkv[:, :width] * scale, qkv[:, width:]], axis=1))
        return 0

    lax.fori_loop(0, cells // block, project, 0)
    low = lax.broadcasted_iota(jnp.int32, (TOKENS, 2 * TOKENS), 1) < TOKENS
    several = HEADS // tiles

    def scores(w, g):
        rows = pl.ds(w, TOKENS, stride=GROUP)
        q = qkv_s[g, rows, :].astype(jnp.bfloat16)
        k = qkv_s[tiles + g, rows, :].astype(jnp.bfloat16)
        keys = jnp.concatenate([k] * several, axis=0) * mask[...]
        return lax.dot_general(
            q, keys, (((1,), (1,)), ((), ())), preferred_element_type=jnp.float32
        )

    def weights(s, g):
        parts = []
        for c in range(several // 2):
            lanes = slice(c * 2 * TOKENS, (c + 1) * 2 * TOKENS)
            start = (g * several // 2 + c) * 2 * TOKENS
            part = s[:, lanes] + bias[:, start : start + 2 * TOKENS]
            one_max = jnp.max(jnp.where(low, part, -jnp.inf), axis=1, keepdims=True)
            two_max = jnp.max(jnp.where(low, -jnp.inf, part), axis=1, keepdims=True)
            parts.append(jnp.exp2(part - jnp.where(low, one_max, two_max)).astype(jnp.bfloat16))
        return jnp.concatenate(parts, axis=1)

    def mix(p, w, g):
        v = qkv_s[2 * tiles + g, pl.ds(w, TOKENS, stride=GROUP), :].astype(jnp.bfloat16)
        vals = jnp.concatenate([v] * several, axis=0) * mask[...]
        return dot(p, jnp.concatenate([vals, mask[...]], axis=1))

    def step(n, _):
        items = [(n * 4 + w, g) for w in range(4) for g in range(tiles)]
        found = [scores(w, g) for w, g in items]
        found = [weights(s, g) for s, (_, g) in zip(found, items)]
        found = [mix(p, w, g) for p, (w, g) in zip(found, items)]
        for both, (w, g) in zip(found, items):
            mix_s[g, pl.ds(w, TOKENS, stride=GROUP), :] = both[:, :lane] / both[:, lane:]
        return 0

    lax.fori_loop(0, GROUP // 4, step, 0)


def feed_forward(blocks, size, x_s, mix_s, out_w, up_w, down_w):
    rows = [pl.ds(pl.multiple_of(i * size, size), size) for i in blocks]
    xs = [get(x_s, r) + dot(get(mix_s, r).astype(jnp.bfloat16), out_w[...]) for r in rows]
    xs = [x.astype(jnp.bfloat16).astype(jnp.float32) for x in xs]
    normed = [norm(x) for x in xs]
    part = 256
    count = up_w.shape[1] // part
    inner = [dot(v, up_w[:, :part]) for v in normed]
    for b in range(count):
        following = inner
        if b + 1 < count:
            following = [dot(v, up_w[:, (b + 1) * part : (b + 2) * part]) for v in normed]
        lines = slice(b * part, (b + 1) * part)
        xs = [
            x + dot(gelu(v.astype(jnp.bfloat16)), down_w[lines, :]) for x, v in zip(xs, inner)
        ]
        inner = following
    return list(zip(blocks, rows, xs))


def neighbours():
    return [(dy, dx) for dy in (-1, 0, 1) for dx in (-1, 0, 1) if dy or dx]


def borders(n_ha, n_wa, field, stage, edge, rows_in, cols_in, corners_in, send_sem, recv_sem):
    rows, cols, _ = field.shape
    my_ha, my_wa = lax.axis_index("ha"), lax.axis_index("wa")
    result = []
    for n, (dy, dx) in enumerate(neighbours()):
        there = (my_ha + dy, my_wa + dx)
        exists = (there[0] >= 0) & (there[0] < n_ha) & (there[1] >= 0) & (there[1] < n_wa)
        from_ha, from_wa = my_ha - dy, my_wa - dx
        comes = (from_ha >= 0) & (from_ha < n_ha) & (from_wa >= 0) & (from_wa < n_wa)
        row = 0 if dy < 0 else rows - 1
        low, left = int(dy < 0), int(dx < 0)
        if dx == 0:
            source, target = field.at[row], rows_in.at[low]
        elif dy == 0:
            source, target = edge.at[1 - left], cols_in.at[left]
        else:
            first = 0 if dx < 0 else cols - GROUP
            source, target = field.at[row, pl.ds(first, GROUP)], corners_in.at[2 * low + left]
        copy = pltpu.make_async_remote_copy(
            src_ref=source,
            dst_ref=target,
            send_sem=send_sem.at[n],
            recv_sem=recv_sem.at[n],
            device_id=there,
            device_id_type=MESH,
        )
        result.append((copy, exists, comes, target))
    return result


def convolve(k, starts, chunk_rows, pitch, stage, expand_w, dw, project_w, hidden, raw, x_s):
    channels = expand_w.shape[-1]
    span = SIDE + 2

    def row(y):
        pieces = []
        for t in range(span):
            for start in starts:
                at = (start + k * chunk_rows + y) * pitch + SIDE - 1 + t
                pieces.append(get(stage, pl.ds(at, SIDE, stride=SIDE)))
        return pieces

    part = 256
    count = channels // part

    def expand(n, _):
        cells = jnp.concatenate(row(2 * n) + row(2 * n + 1), axis=0)
        raw[pl.ds(2 * n, 2)] = cells.reshape(2, span, GROUP, cells.shape[1]).astype(jnp.bfloat16)
        normed = norm(cells)
        inner = dot(normed, expand_w[:, :part])
        for b in range(count):
            following = inner
            if b + 1 < count:
                following = dot(normed, expand_w[:, (b + 1) * part : (b + 2) * part])
            hidden[pl.ds(2 * n, 2), :, :, b * part : (b + 1) * part] = gelu(
                inner.astype(jnp.bfloat16)
            ).reshape(2, span, GROUP, part)
            inner = following
        return 0

    lax.fori_loop(0, span // 2, expand, 0)
    size = 2 * SIDE * GROUP

    def depthwise(n, _):
        x = raw[pl.ds(2 * n + 1, 2), 1 : 1 + SIDE].astype(jnp.float32).reshape(size, raw.shape[3])
        for b in range(count):
            lanes = slice(b * part, (b + 1) * part)
            both = []
            for y in (2 * n, 2 * n + 1):
                total = None
                for dy in range(3):
                    for dx in range(3):
                        term = (
                            hidden[y + dy, dx : dx + SIDE, :, lanes]
                            * dw[3 * dy + dx, :, lanes][None]
                        )
                        total = term if total is None else total + term
                both.append(gelu(total).reshape(size // 2, part))
            x = x + dot(jnp.concatenate(both, axis=0), project_w[lanes, :])
        rows = pl.ds(pl.multiple_of(n * size, size), size)
        put(x_s, rows, x.astype(jnp.bfloat16).astype(jnp.float32))
        return 0

    lax.fori_loop(0, SIDE // 2, depthwise, 0)


def layer_kernel(
    lead, n_ha, n_wa, part_rows, part_cols, starts, chunk_rows,
    field, expand_w, dw_kernel, project_w, blk_qkv, blk_out, blk_bias, blk_up, blk_down,
    grid_qkv, grid_out, grid_bias, grid_up, grid_down,
    out,
    stage, edge, rows_in, cols_in, corners_in, mask, dw, edge_send, edge_recv,
    hidden, raw, x_s, qkv_s, mix_s, ready, arrived, result,
    send_go, recv_go, send_back, recv_back,
):
    chunks, devices, per, width = out.shape
    my_ha, my_wa = lax.axis_index("ha"), lax.axis_index("wa")
    me = my_ha * n_wa + my_wa
    blocks = SIDE // part_rows
    size = part_rows * SIDE * GROUP
    share = devices // blocks
    lines = part_rows * part_cols

    barrier = pltpu.get_barrier_semaphore()

    def greet(o, _):
        d = lax.rem(me + o, devices)
        pl.semaphore_signal(
            barrier, inc=1, device_id=(d // n_wa, lax.rem(d, n_wa)), device_id_type=MESH
        )
        return 0

    lax.fori_loop(1, devices, greet, 0)

    rows, cols, _ = field.shape
    pitch = cols + 2 * SIDE

    def lay(y, _):
        at = pl.ds(pl.multiple_of((y + 1) * pitch + SIDE, SIDE), cols)
        put(stage, at, field[y].astype(jnp.float32))
        return 0

    lax.fori_loop(0, rows, lay, 0)
    edge[0] = get(stage, pl.ds(pitch + SIDE, rows, stride=pitch)).astype(jnp.bfloat16)
    edge[1] = get(stage, pl.ds(pitch + SIDE + cols - 1, rows, stride=pitch)).astype(jnp.bfloat16)
    pl.semaphore_wait(barrier, devices - 1)
    crossings = borders(
        n_ha, n_wa, field, stage, edge, rows_in, cols_in, corners_in, edge_send, edge_recv
    )
    for copy, exists, _, _ in crossings:
        pl.when(exists)(copy.start)
    mask[...] = (
        (lax.broadcasted_iota(jnp.int32, mask.shape, 0) // TOKENS)
        == (lax.broadcasted_iota(jnp.int32, mask.shape, 1) // (width // HEADS))
    ).astype(jnp.float32).astype(jnp.bfloat16)
    for tap in range(9):
        dw[tap] = jnp.broadcast_to(dw_kernel[tap : tap + 1, :], dw.shape[1:]).astype(jnp.bfloat16)
    for copy, exists, comes, target in crossings:
        @pl.when(jnp.logical_not(comes))
        def _():
            target[...] = jnp.zeros(target.shape, jnp.bfloat16)

        pl.when(comes)(copy.wait_recv)
        pl.when(exists)(copy.wait_send)
    bottom = (rows + 1) * pitch
    put(stage, slice(SIDE, SIDE + cols), rows_in[0].astype(jnp.float32))
    put(stage, slice(bottom + SIDE, bottom + SIDE + cols), rows_in[1].astype(jnp.float32))
    left, right = SIDE - 1, SIDE + cols
    put(stage, pl.ds(pitch + left, rows, stride=pitch), cols_in[0].astype(jnp.float32))
    put(stage, pl.ds(pitch + right, rows, stride=pitch), cols_in[1].astype(jnp.float32))
    for n, (at, line) in enumerate(
        [(left, GROUP - 1), (right, 0), (bottom + left, GROUP - 1), (bottom + right, 0)]
    ):
        cell = corners_in[n].astype(jnp.float32)[line : line + 1]
        put(stage, slice(at, at + 1), cell)

    def ship(k, d, source, target, send_sem, recv_sem):
        @pl.when(d != me)
        def _():
            pltpu.make_async_remote_copy(
                src_ref=source.at[k, d],
                dst_ref=target.at[k, me],
                send_sem=send_sem.at[k],
                recv_sem=recv_sem.at[k],
                device_id=(d // n_wa, lax.rem(d, n_wa)),
                device_id_type=MESH,
            ).start()

        @pl.when(d == me)
        def _():
            target[k, d] = source[k, d]

    def all_of(k, source, target, send_sem, recv_sem):
        other = lax.rem(me + 1, devices)
        return pltpu.make_async_remote_copy(
            src_ref=source.at[k, pl.ds(0, devices - 1)],
            dst_ref=target.at[k, pl.ds(0, devices - 1)],
            send_sem=send_sem.at[k],
            recv_sem=recv_sem.at[k],
            device_id=(other // n_wa, lax.rem(other, n_wa)),
            device_id_type=MESH,
        )

    def block_chunk(k, _):
        convolve(
            k, starts, chunk_rows, pitch, stage, expand_w, dw, project_w, hidden, raw, x_s
        )
        attention(x_s, qkv_s, mix_s, blk_qkv, blk_bias, mask)

        def send(i, rows, value):
            put(x_s, rows, value)
            for w in range(GROUP):
                strip, square = w // SIDE, w % SIDE
                for h in range(SIDE // part_cols):
                    first = i * size + h * part_cols * GROUP + w
                    if part_cols == SIDE:
                        piece = get(x_s, pl.ds(first, lines, stride=GROUP))
                    else:
                        piece = jnp.concatenate(
                            [
                                get(
                                    x_s,
                                    pl.ds(first + r * SIDE * GROUP, part_cols, stride=GROUP),
                                )
                                for r in range(part_rows)
                            ],
                            axis=0,
                        )
                    piece = piece.astype(jnp.bfloat16)
                    if lead == 2:
                        ready[k, i * n_wa + square, strip * lines : (strip + 1) * lines] = piece
                    else:
                        row = strip * blocks + i
                        ready[k, row * n_wa + square * (SIDE // part_cols) + h] = piece

            def go(o, _):
                d = lax.rem(my_wa + o, n_wa)
                for strip in range(2 // lead):
                    ship(
                        k, (strip * blocks + i) * n_wa + d, ready, arrived, send_go, recv_go
                    )
                return 0

            lax.fori_loop(0, n_wa, go, 0)

        def step(n, _):
            pair = [lax.rem(2 * n + my_ha + 1 + o, blocks) for o in range(2)]
            done = feed_forward(pair, size, x_s, mix_s, blk_out, blk_up, blk_down)
            for i, rows, value in done:
                send(i, rows, value)
            return 0

        lax.fori_loop(0, blocks // 2, step, 0)
        return 0

    lax.fori_loop(0, chunks, block_chunk, 0)

    def grid_chunk(k, _):
        all_of(k, ready, arrived, send_go, recv_go).wait_recv()
        put(x_s, slice(None), arrived[k].astype(jnp.float32).reshape(devices * per, width))
        attention(x_s, qkv_s, mix_s, grid_qkv, grid_bias, mask)

        def send(i, value):
            first = pl.multiple_of(i * share, share)
            result[k, pl.ds(first, share)] = value.reshape(share, per, width).astype(jnp.bfloat16)

            def go(o, _):
                d = i * share + lax.rem(my_wa + o, share)
                ship(k, d, result, out, send_back, recv_back)
                return 0

            lax.fori_loop(0, share, go, 0)

        def step(n, _):
            pair = [lax.rem(2 * n + my_ha + 1 + o, blocks) for o in range(2)]
            done = feed_forward(pair, size, x_s, mix_s, grid_out, grid_up, grid_down)
            for i, _, value in done:
                send(i, value)
            return 0

        lax.fori_loop(0, blocks // 2, step, 0)
        return 0

    lax.fori_loop(0, chunks, grid_chunk, 0)

    def finish(k, _):
        all_of(k, ready, arrived, send_go, recv_go).wait_send()
        all_of(k, result, out, send_back, recv_back).wait()
        return 0

    lax.fori_loop(0, chunks, finish, 0)


def bias_kernel(lead, tables, blk_index, grid_index, *outs):
    token = lax.broadcasted_iota(jnp.int32, (TOKENS, TOKENS), 0)
    position = lax.broadcasted_iota(jnp.int32, (TOKENS, TOKENS), 1)
    span = SIDE * lead
    inside = lax.rem(token, span)
    wanted = token - inside + SIDE * lax.rem(inside, lead) + lax.div(inside, lead)
    order = (wanted == position).astype(jnp.float32)
    ordered = lax.dot_general(
        dot(order, grid_index[...].astype(jnp.float32)),
        order,
        (((1,), (1,)), ((), ())),
        preferred_element_type=jnp.float32,
    )
    indices = [blk_index[...], (ordered + 0.5).astype(jnp.int32)]
    low = lax.broadcasted_iota(jnp.int32, (TOKENS, 2 * TOKENS), 1) < TOKENS
    for a in range(2):
        index = jnp.concatenate([indices[a], indices[a]], axis=1)
        within = index % 128
        upper = index >= 128
        found = []
        for h in range(HEADS):
            halves = [
                jnp.take_along_axis(
                    jnp.broadcast_to(tables[a, h : h + 1, n * 128 : (n + 1) * 128], index.shape),
                    within,
                    axis=1,
                    mode="promise_in_bounds",
                )
                for n in range(2)
            ]
            found.append(jnp.where(upper, halves[1], halves[0]))
        for c in range(HEADS // 2):
            outs[a][:, c * 2 * TOKENS : (c + 1) * 2 * TOKENS] = (
                jnp.where(low, found[2 * c], found[2 * c + 1]) * LOG2E
            )


def on_device(
    field,
    expand_w,
    dw_kernel,
    project_w,
    blk_qkv,
    blk_out,
    blk_table,
    blk_index,
    blk_up,
    blk_down,
    grid_qkv,
    grid_out,
    grid_table,
    grid_index,
    grid_up,
    grid_down,
):
    rows, cols, width = field.shape
    channels = expand_w.shape[1]
    n_ha = lax.axis_size("ha")
    n_wa = lax.axis_size("wa")
    lead = SIDE // n_ha
    stride_rows = rows // lead
    chunks = rows // (2 * SIDE)
    chunk_rows = stride_rows // chunks
    part_rows = chunk_rows // n_ha
    part_cols = cols // n_wa
    strips = 2
    cells = GROUP * TOKENS

    tables = jnp.stack([blk_table, grid_table]).transpose(0, 2, 1)
    tables = jnp.pad(tables, ((0, 0), (0, 0), (0, 256 - tables.shape[2])))
    bias = pl.pallas_call(
        functools.partial(bias_kernel, lead),
        out_shape=[jax.ShapeDtypeStruct((TOKENS, HEADS * TOKENS), jnp.float32)] * 2,
    )(tables, blk_index, grid_index)
    per = cells // (n_ha * n_wa)
    starts = [
        (m // (strips // lead)) * stride_rows + (m % (strips // lead)) * SIDE
        for m in range(strips)
    ]
    pitch = cols + 2 * SIDE
    parts = (chunks, n_ha * n_wa, per, width)
    layer = pl.pallas_call(
        functools.partial(
            layer_kernel, lead, n_ha, n_wa, part_rows, part_cols, starts, chunk_rows
        ),
        out_shape=jax.ShapeDtypeStruct(parts, jnp.bfloat16),
        in_specs=[pl.BlockSpec(memory_space=pltpu.VMEM)] * 14,
        out_specs=pl.BlockSpec(memory_space=pltpu.VMEM),
        scratch_shapes=[
            pltpu.VMEM((width // 128, (rows + 2) * pitch, 128), jnp.float32),
            pltpu.VMEM((2, rows, width), jnp.bfloat16),
            pltpu.VMEM((2, cols, width), jnp.bfloat16),
            pltpu.VMEM((2, rows, width), jnp.bfloat16),
            pltpu.VMEM((4, GROUP, width), jnp.bfloat16),
            pltpu.VMEM((HEADS * TOKENS * 128 // width, 128), jnp.bfloat16),
            pltpu.VMEM((9, GROUP, channels), jnp.bfloat16),
            pltpu.SemaphoreType.DMA((8,)),
            pltpu.SemaphoreType.DMA((8,)),
            pltpu.VMEM((SIDE + 2, SIDE + 2, GROUP, channels), jnp.bfloat16),
            pltpu.VMEM((SIDE + 2, SIDE + 2, GROUP, width), jnp.bfloat16),
            pltpu.VMEM((width // 128, cells, 128), jnp.float32),
            pltpu.VMEM((3 * width // 128, cells, 128), jnp.float32),
            pltpu.VMEM((width // 128, cells, 128), jnp.float32),
            pltpu.VMEM(parts, jnp.bfloat16),
            pltpu.VMEM(parts, jnp.bfloat16),
            pltpu.VMEM(parts, jnp.bfloat16),
        ]
        + [pltpu.SemaphoreType.DMA((chunks,))] * 4,
        compiler_params=pltpu.CompilerParams(
            vmem_limit_bytes=VMEM_LIMIT, collective_id=0, has_side_effects=True
        ),
        cost_estimate=pl.CostEstimate(
            flops=2 * rows * cols * width * 36 * width, bytes_accessed=12 << 20, transcendentals=0
        ),
    )
    back = layer(
        field, expand_w, dw_kernel, project_w, blk_qkv, blk_out, bias[0], blk_up, blk_down,
        grid_qkv, grid_out, bias[1], grid_up, grid_down,
    )
    updated = back.reshape(chunks, n_ha, n_wa, lead, part_rows, part_cols, width)
    return updated.transpose(3, 0, 1, 4, 2, 5, 6).reshape(rows, cols, width)


def solution(mesh):
    placed = (P("ha", "wa", None),) + (P(),) * 15
    return jax.shard_map(
        on_device, mesh=mesh, in_specs=placed, out_specs=P("ha", "wa", None), check_vma=False
    )
```

```python
import functools
import math

import jax
import jax.numpy as jnp
from jax import lax
from jax.experimental import pallas as pl
from jax.experimental.pallas import tpu as pltpu
from jax.sharding import PartitionSpec as P

EPS = 1e-05
HEADS = 8
SIDE = 8
TOKENS = SIDE * SIDE
GROUP = 16
LOG2E = math.log2(math.e)
MESH = pl.DeviceIdType.MESH
VMEM_LIMIT = 56 * 1024 * 1024


def norm(wide):
    center = wide - jnp.mean(wide, axis=-1, keepdims=True)
    spread = jnp.mean(center * center, axis=-1, keepdims=True)
    return (center * lax.rsqrt(spread + EPS)).astype(jnp.bfloat16)


def gelu(v):
    kind = v.dtype
    first = jnp.asarray(math.sqrt(2 / math.pi), kind)
    third = jnp.asarray(math.sqrt(2 / math.pi) * 0.044715, kind)
    half = jnp.asarray(0.5, kind) * v
    return half + half * jnp.tanh(v * (first + third * (v * v)))


def put(ref, rows, value):
    for c in range(value.shape[1] // 128):
        ref[c, rows, :] = value[:, c * 128 : (c + 1) * 128]


def get(ref, rows, first=0, last=None):
    last = ref.shape[0] if last is None else last
    return jnp.concatenate([ref[c, rows, :] for c in range(first, last)], axis=1)


def dot(a, b):
    return jnp.dot(a, b, preferred_element_type=jnp.float32)


def attention(x_s, qkv_s, mix_s, qkv_w, bias, mask):
    tiles, cells, lane = x_s.shape
    width = tiles * lane
    block = 512
    scale = LOG2E / math.sqrt(width // HEADS)

    def project(i, _):
        rows = pl.ds(pl.multiple_of(i * block, block), block)
        qkv = dot(norm(get(x_s, rows)), qkv_w[...])
        put(qkv_s, rows, jnp.concatenate([qkv[:, :width] * scale, qkv[:, width:]], axis=1))
        return 0

    lax.fori_loop(0, cells // block, project, 0)
    low = lax.broadcasted_iota(jnp.int32, (TOKENS, 2 * TOKENS), 1) < TOKENS
    several = HEADS // tiles

    def scores(w, g):
        rows = pl.ds(w, TOKENS, stride=GROUP)
        q = qkv_s[g, rows, :].astype(jnp.bfloat16)
        k = qkv_s[tiles + g, rows, :].astype(jnp.bfloat16)
        keys = jnp.concatenate([k] * several, axis=0) * mask[...]
        return lax.dot_general(
            q, keys, (((1,), (1,)), ((), ())), preferred_element_type=jnp.float32
        )

    def weights(s, g):
        parts = []
        for c in range(several // 2):
            lanes = slice(c * 2 * TOKENS, (c + 1) * 2 * TOKENS)
            start = (g * several // 2 + c) * 2 * TOKENS
            part = s[:, lanes] + bias[:, start : start + 2 * TOKENS]
            one_max = jnp.max(jnp.where(low, part, -jnp.inf), axis=1, keepdims=True)
            two_max = jnp.max(jnp.where(low, -jnp.inf, part), axis=1, keepdims=True)
            parts.append(jnp.exp2(part - jnp.where(low, one_max, two_max)).astype(jnp.bfloat16))
        return jnp.concatenate(parts, axis=1)

    def mix(p, w, g):
        v = qkv_s[2 * tiles + g, pl.ds(w, TOKENS, stride=GROUP), :].astype(jnp.bfloat16)
        vals = jnp.concatenate([v] * several, axis=0) * mask[...]
        return dot(p, jnp.concatenate([vals, mask[...]], axis=1))

    def step(n, _):
        items = [(n * 4 + w, g) for w in range(4) for g in range(tiles)]
        found = [scores(w, g) for w, g in items]
        found = [weights(s, g) for s, (_, g) in zip(found, items)]
        found = [mix(p, w, g) for p, (w, g) in zip(found, items)]
        for both, (w, g) in zip(found, items):
            mix_s[g, pl.ds(w, TOKENS, stride=GROUP), :] = both[:, :lane] / both[:, lane:]
        return 0

    lax.fori_loop(0, GROUP // 4, step, 0)


def feed_forward(blocks, size, x_s, mix_s, out_w, up_w, down_w):
    rows = [pl.ds(pl.multiple_of(i * size, size), size) for i in blocks]
    xs = [get(x_s, r) + dot(get(mix_s, r).astype(jnp.bfloat16), out_w[...]) for r in rows]
    xs = [x.astype(jnp.bfloat16).astype(jnp.float32) for x in xs]
    normed = [norm(x) for x in xs]
    part = 256
    count = up_w.shape[1] // part
    inner = [dot(v, up_w[:, :part]) for v in normed]
    for b in range(count):
        following = inner
        if b + 1 < count:
            following = [dot(v, up_w[:, (b + 1) * part : (b + 2) * part]) for v in normed]
        lines = slice(b * part, (b + 1) * part)
        xs = [
            x + dot(gelu(v.astype(jnp.bfloat16)), down_w[lines, :]) for x, v in zip(xs, inner)
        ]
        inner = following
    return list(zip(blocks, rows, xs))


def neighbours():
    return [(dy, dx) for dy in (-1, 0, 1) for dx in (-1, 0, 1) if dy or dx]


def borders(n_ha, n_wa, field, stage, edge, rows_in, cols_in, corners_in, send_sem, recv_sem):
    rows, cols, _ = field.shape
    my_ha, my_wa = lax.axis_index("ha"), lax.axis_index("wa")
    result = []
    for n, (dy, dx) in enumerate(neighbours()):
        there = (my_ha + dy, my_wa + dx)
        exists = (there[0] >= 0) & (there[0] < n_ha) & (there[1] >= 0) & (there[1] < n_wa)
        from_ha, from_wa = my_ha - dy, my_wa - dx
        comes = (from_ha >= 0) & (from_ha < n_ha) & (from_wa >= 0) & (from_wa < n_wa)
        row = 0 if dy < 0 else rows - 1
        low, left = int(dy < 0), int(dx < 0)
        if dx == 0:
            source, target = field.at[row], rows_in.at[low]
        elif dy == 0:
            source, target = edge.at[1 - left], cols_in.at[left]
        else:
            first = 0 if dx < 0 else cols - GROUP
            source, target = field.at[row, pl.ds(first, GROUP)], corners_in.at[2 * low + left]
        copy = pltpu.make_async_remote_copy(
            src_ref=source,
            dst_ref=target,
            send_sem=send_sem.at[n],
            recv_sem=recv_sem.at[n],
            device_id=there,
            device_id_type=MESH,
        )
        result.append((copy, exists, comes, target))
    return result


def convolve(k, starts, chunk_rows, pitch, stage, expand_w, dw, project_w, hidden, raw, x_s):
    channels = expand_w.shape[-1]
    span = SIDE + 2

    def row(y):
        pieces = []
        for t in range(span):
            for start in starts:
                at = (start + k * chunk_rows + y) * pitch + SIDE - 1 + t
                pieces.append(get(stage, pl.ds(at, SIDE, stride=SIDE)))
        return pieces

    part = 256
    count = channels // part

    def expand(n, _):
        cells = jnp.concatenate(row(2 * n) + row(2 * n + 1), axis=0)
        raw[pl.ds(2 * n, 2)] = cells.reshape(2, span, GROUP, cells.shape[1]).astype(jnp.bfloat16)
        normed = norm(cells)
        inner = dot(normed, expand_w[:, :part])
        for b in range(count):
            following = inner
            if b + 1 < count:
                following = dot(normed, expand_w[:, (b + 1) * part : (b + 2) * part])
            hidden[pl.ds(2 * n, 2), :, :, b * part : (b + 1) * part] = gelu(
                inner.astype(jnp.bfloat16)
            ).reshape(2, span, GROUP, part)
            inner = following
        return 0

    lax.fori_loop(0, span // 2, expand, 0)
    size = 2 * SIDE * GROUP

    def depthwise(n, _):
        x = raw[pl.ds(2 * n + 1, 2), 1 : 1 + SIDE].astype(jnp.float32).reshape(size, raw.shape[3])
        for b in range(count):
            lanes = slice(b * part, (b + 1) * part)
            both = []
            for y in (2 * n, 2 * n + 1):
                total = None
                for dy in range(3):
                    for dx in range(3):
                        term = (
                            hidden[y + dy, dx : dx + SIDE, :, lanes]
                            * dw[3 * dy + dx, :, lanes][None]
                        )
                        total = term if total is None else total + term
                both.append(gelu(total).reshape(size // 2, part))
            x = x + dot(jnp.concatenate(both, axis=0), project_w[lanes, :])
        rows = pl.ds(pl.multiple_of(n * size, size), size)
        put(x_s, rows, x.astype(jnp.bfloat16).astype(jnp.float32))
        return 0

    lax.fori_loop(0, SIDE // 2, depthwise, 0)


def layer_kernel(
    lead, n_ha, n_wa, part_rows, part_cols, starts, chunk_rows,
    field, expand_w, dw_kernel, project_w, blk_qkv, blk_out, blk_bias, blk_up, blk_down,
    grid_qkv, grid_out, grid_bias, grid_up, grid_down,
    out,
    stage, edge, rows_in, cols_in, corners_in, mask, dw, edge_send, edge_recv,
    hidden, raw, x_s, qkv_s, mix_s, ready, arrived, result,
    send_go, recv_go, send_back, recv_back,
):
    chunks, devices, per, width = out.shape
    my_ha, my_wa = lax.axis_index("ha"), lax.axis_index("wa")
    me = my_ha * n_wa + my_wa
    blocks = SIDE // part_rows
    size = part_rows * SIDE * GROUP
    share = devices // blocks
    lines = part_rows * part_cols

    barrier = pltpu.get_barrier_semaphore()

    def greet(o, _):
        d = lax.rem(me + o, devices)
        pl.semaphore_signal(
            barrier, inc=1, device_id=(d // n_wa, lax.rem(d, n_wa)), device_id_type=MESH
        )
        return 0

    lax.fori_loop(1, devices, greet, 0)

    rows, cols, _ = field.shape
    pitch = cols + 2 * SIDE

    def lay(y, _):
        at = pl.ds(pl.multiple_of((y + 1) * pitch + SIDE, SIDE), cols)
        put(stage, at, field[y].astype(jnp.float32))
        return 0

    lax.fori_loop(0, rows, lay, 0)
    edge[0] = get(stage, pl.ds(pitch + SIDE, rows, stride=pitch)).astype(jnp.bfloat16)
    edge[1] = get(stage, pl.ds(pitch + SIDE + cols - 1, rows, stride=pitch)).astype(jnp.bfloat16)
    pl.semaphore_wait(barrier, devices - 1)
    crossings = borders(
        n_ha, n_wa, field, stage, edge, rows_in, cols_in, corners_in, edge_send, edge_recv
    )
    for copy, exists, _, _ in crossings:
        pl.when(exists)(copy.start)
    mask[...] = (
        (lax.broadcasted_iota(jnp.int32, mask.shape, 0) // TOKENS)
        == (lax.broadcasted_iota(jnp.int32, mask.shape, 1) // (width // HEADS))
    ).astype(jnp.float32).astype(jnp.bfloat16)
    for tap in range(9):
        dw[tap] = jnp.broadcast_to(dw_kernel[tap : tap + 1, :], dw.shape[1:]).astype(jnp.bfloat16)
    for copy, exists, comes, target in crossings:
        @pl.when(jnp.logical_not(comes))
        def _():
            target[...] = jnp.zeros(target.shape, jnp.bfloat16)

        pl.when(comes)(copy.wait_recv)
        pl.when(exists)(copy.wait_send)
    bottom = (rows + 1) * pitch
    put(stage, slice(SIDE, SIDE + cols), rows_in[0].astype(jnp.float32))
    put(stage, slice(bottom + SIDE, bottom + SIDE + cols), rows_in[1].astype(jnp.float32))
    left, right = SIDE - 1, SIDE + cols
    put(stage, pl.ds(pitch + left, rows, stride=pitch), cols_in[0].astype(jnp.float32))
    put(stage, pl.ds(pitch + right, rows, stride=pitch), cols_in[1].astype(jnp.float32))
    for n, (at, line) in enumerate(
        [(left, GROUP - 1), (right, 0), (bottom + left, GROUP - 1), (bottom + right, 0)]
    ):
        cell = corners_in[n].astype(jnp.float32)[line : line + 1]
        put(stage, slice(at, at + 1), cell)

    def ship(k, d, source, target, send_sem, recv_sem):
        @pl.when(d != me)
        def _():
            pltpu.make_async_remote_copy(
                src_ref=source.at[k, d],
                dst_ref=target.at[k, me],
                send_sem=send_sem.at[k],
                recv_sem=recv_sem.at[k],
                device_id=(d // n_wa, lax.rem(d, n_wa)),
                device_id_type=MESH,
            ).start()

        @pl.when(d == me)
        def _():
            target[k, d] = source[k, d]

    def all_of(k, source, target, send_sem, recv_sem):
        other = lax.rem(me + 1, devices)
        return pltpu.make_async_remote_copy(
            src_ref=source.at[k, pl.ds(0, devices - 1)],
            dst_ref=target.at[k, pl.ds(0, devices - 1)],
            send_sem=send_sem.at[k],
            recv_sem=recv_sem.at[k],
            device_id=(other // n_wa, lax.rem(other, n_wa)),
            device_id_type=MESH,
        )

    def block_chunk(k, _):
        convolve(
            k, starts, chunk_rows, pitch, stage, expand_w, dw, project_w, hidden, raw, x_s
        )
        attention(x_s, qkv_s, mix_s, blk_qkv, blk_bias, mask)

        def send(i, rows, value):
            put(x_s, rows, value)
            for w in range(GROUP):
                strip, square = w // SIDE, w % SIDE
                for h in range(SIDE // part_cols):
                    first = i * size + h * part_cols * GROUP + w
                    if part_cols == SIDE:
                        piece = get(x_s, pl.ds(first, lines, stride=GROUP))
                    else:
                        piece = jnp.concatenate(
                            [
                                get(
                                    x_s,
                                    pl.ds(first + r * SIDE * GROUP, part_cols, stride=GROUP),
                                )
                                for r in range(part_rows)
                            ],
                            axis=0,
                        )
                    piece = piece.astype(jnp.bfloat16)
                    if lead == 2:
                        ready[k, i * n_wa + square, strip * lines : (strip + 1) * lines] = piece
                    else:
                        row = strip * blocks + i
                        ready[k, row * n_wa + square * (SIDE // part_cols) + h] = piece

            def go(o, _):
                d = lax.rem(my_wa + o, n_wa)
                for strip in range(2 // lead):
                    ship(
                        k, (strip * blocks + i) * n_wa + d, ready, arrived, send_go, recv_go
                    )
                return 0

            lax.fori_loop(0, n_wa, go, 0)

        def step(n, _):
            pair = [lax.rem(2 * n + my_ha + 1 + o, blocks) for o in range(2)]
            done = feed_forward(pair, size, x_s, mix_s, blk_out, blk_up, blk_down)
            for i, rows, value in done:
                send(i, rows, value)
            return 0

        lax.fori_loop(0, blocks // 2, step, 0)
        return 0

    block_chunk(0, 0)

    def grid_chunk(k, _):
        all_of(k, ready, arrived, send_go, recv_go).wait_recv()
        put(x_s, slice(None), arrived[k].astype(jnp.float32).reshape(devices * per, width))
        attention(x_s, qkv_s, mix_s, grid_qkv, grid_bias, mask)

        def send(i, value):
            first = pl.multiple_of(i * share, share)
            result[k, pl.ds(first, share)] = value.reshape(share, per, width).astype(jnp.bfloat16)

            def go(o, _):
                d = i * share + lax.rem(my_wa + o, share)
                ship(k, d, result, out, send_back, recv_back)
                return 0

            lax.fori_loop(0, share, go, 0)

        def step(n, _):
            pair = [lax.rem(2 * n + my_ha + 1 + o, blocks) for o in range(2)]
            done = feed_forward(pair, size, x_s, mix_s, grid_out, grid_up, grid_down)
            for i, _, value in done:
                send(i, value)
            return 0

        lax.fori_loop(0, blocks // 2, step, 0)
        return 0

    def both(k, _):
        block_chunk(k, 0)
        grid_chunk(k - 1, 0)
        return 0

    lax.fori_loop(1, chunks, both, 0)
    grid_chunk(chunks - 1, 0)

    def finish(k, _):
        all_of(k, ready, arrived, send_go, recv_go).wait_send()
        all_of(k, result, out, send_back, recv_back).wait()
        return 0

    lax.fori_loop(0, chunks, finish, 0)


def bias_kernel(lead, tables, blk_index, grid_index, *outs):
    token = lax.broadcasted_iota(jnp.int32, (TOKENS, TOKENS), 0)
    position = lax.broadcasted_iota(jnp.int32, (TOKENS, TOKENS), 1)
    span = SIDE * lead
    inside = lax.rem(token, span)
    wanted = token - inside + SIDE * lax.rem(inside, lead) + lax.div(inside, lead)
    order = (wanted == position).astype(jnp.float32)
    ordered = lax.dot_general(
        dot(order, grid_index[...].astype(jnp.float32)),
        order,
        (((1,), (1,)), ((), ())),
        preferred_element_type=jnp.float32,
    )
    indices = [blk_index[...], (ordered + 0.5).astype(jnp.int32)]
    low = lax.broadcasted_iota(jnp.int32, (TOKENS, 2 * TOKENS), 1) < TOKENS
    for a in range(2):
        index = jnp.concatenate([indices[a], indices[a]], axis=1)
        within = index % 128
        upper = index >= 128
        found = []
        for h in range(HEADS):
            halves = [
                jnp.take_along_axis(
                    jnp.broadcast_to(tables[a, h : h + 1, n * 128 : (n + 1) * 128], index.shape),
                    within,
                    axis=1,
                    mode="promise_in_bounds",
                )
                for n in range(2)
            ]
            found.append(jnp.where(upper, halves[1], halves[0]))
        for c in range(HEADS // 2):
            outs[a][:, c * 2 * TOKENS : (c + 1) * 2 * TOKENS] = (
                jnp.where(low, found[2 * c], found[2 * c + 1]) * LOG2E
            )


def on_device(
    field,
    expand_w,
    dw_kernel,
    project_w,
    blk_qkv,
    blk_out,
    blk_table,
    blk_index,
    blk_up,
    blk_down,
    grid_qkv,
    grid_out,
    grid_table,
    grid_index,
    grid_up,
    grid_down,
):
    rows, cols, width = field.shape
    channels = expand_w.shape[1]
    n_ha = lax.axis_size("ha")
    n_wa = lax.axis_size("wa")
    lead = SIDE // n_ha
    stride_rows = rows // lead
    chunks = rows // (2 * SIDE)
    chunk_rows = stride_rows // chunks
    part_rows = chunk_rows // n_ha
    part_cols = cols // n_wa
    strips = 2
    cells = GROUP * TOKENS

    tables = jnp.stack([blk_table, grid_table]).transpose(0, 2, 1)
    tables = jnp.pad(tables, ((0, 0), (0, 0), (0, 256 - tables.shape[2])))
    bias = pl.pallas_call(
        functools.partial(bias_kernel, lead),
        out_shape=[jax.ShapeDtypeStruct((TOKENS, HEADS * TOKENS), jnp.float32)] * 2,
    )(tables, blk_index, grid_index)
    per = cells // (n_ha * n_wa)
    starts = [
        (m // (strips // lead)) * stride_rows + (m % (strips // lead)) * SIDE
        for m in range(strips)
    ]
    pitch = cols + 2 * SIDE
    parts = (chunks, n_ha * n_wa, per, width)
    layer = pl.pallas_call(
        functools.partial(
            layer_kernel, lead, n_ha, n_wa, part_rows, part_cols, starts, chunk_rows
        ),
        out_shape=jax.ShapeDtypeStruct(parts, jnp.bfloat16),
        in_specs=[pl.BlockSpec(memory_space=pltpu.VMEM)] * 14,
        out_specs=pl.BlockSpec(memory_space=pltpu.VMEM),
        scratch_shapes=[
            pltpu.VMEM((width // 128, (rows + 2) * pitch, 128), jnp.float32),
            pltpu.VMEM((2, rows, width), jnp.bfloat16),
            pltpu.VMEM((2, cols, width), jnp.bfloat16),
            pltpu.VMEM((2, rows, width), jnp.bfloat16),
            pltpu.VMEM((4, GROUP, width), jnp.bfloat16),
            pltpu.VMEM((HEADS * TOKENS * 128 // width, 128), jnp.bfloat16),
            pltpu.VMEM((9, GROUP, channels), jnp.bfloat16),
            pltpu.SemaphoreType.DMA((8,)),
            pltpu.SemaphoreType.DMA((8,)),
            pltpu.VMEM((SIDE + 2, SIDE + 2, GROUP, channels), jnp.bfloat16),
            pltpu.VMEM((SIDE + 2, SIDE + 2, GROUP, width), jnp.bfloat16),
            pltpu.VMEM((width // 128, cells, 128), jnp.float32),
            pltpu.VMEM((3 * width // 128, cells, 128), jnp.float32),
            pltpu.VMEM((width // 128, cells, 128), jnp.float32),
            pltpu.VMEM(parts, jnp.bfloat16),
            pltpu.VMEM(parts, jnp.bfloat16),
            pltpu.VMEM(parts, jnp.bfloat16),
        ]
        + [pltpu.SemaphoreType.DMA((chunks,))] * 4,
        compiler_params=pltpu.CompilerParams(
            vmem_limit_bytes=VMEM_LIMIT, collective_id=0, has_side_effects=True
        ),
        cost_estimate=pl.CostEstimate(
            flops=2 * rows * cols * width * 36 * width, bytes_accessed=12 << 20, transcendentals=0
        ),
    )
    back = layer(
        field, expand_w, dw_kernel, project_w, blk_qkv, blk_out, bias[0], blk_up, blk_down,
        grid_qkv, grid_out, bias[1], grid_up, grid_down,
    )
    updated = back.reshape(chunks, n_ha, n_wa, lead, part_rows, part_cols, width)
    return updated.transpose(3, 0, 1, 4, 2, 5, 6).reshape(rows, cols, width)


def solution(mesh):
    placed = (P("ha", "wa", None),) + (P(),) * 15
    return jax.shard_map(
        on_device, mesh=mesh, in_specs=placed, out_specs=P("ha", "wa", None), check_vma=False
    )
```
